128 devices in a mesh: req: 16 (over y, x), kvh: 8 (over z, core).
Axes of the slice: x: 4, y: 4, z: 4, core: 2. Of those that a mesh axis runs over, the one named last changes fastest.
Arguments:
- queries: bfloat16 [256, 8192], P('req', 'kvh'), may hold values from -150 to 150
- corpus_keys: bfloat16 [65536, 1024], P('req', 'kvh'), may hold values from -6 to 6
- corpus_values: bfloat16 [65536, 1024], P('req', 'kvh'), may hold values from -6 to 6
- task_keys: bfloat16 [32768, 1024], P('req', 'kvh'), may hold values from -7 to 7
- task_values: bfloat16 [32768, 1024], P('req', 'kvh'), may hold values from -6 to 6
- history_keys: bfloat16 [131072, 1024], P('req', 'kvh'), may hold values from -8 to 8
- history_values: bfloat16 [131072, 1024], P('req', 'kvh'), may hold values from -6 to 6
- history_lengths: int32 [256], P('req'), may hold values from 1 to 512, as said below
- task_of: int32 [256], replicated, may hold values from 0 to 7
- out_weight: bfloat16 [8192, 8192], P('kvh'), may hold values from -0.0625 to 0.0625
Outputs:
- mixed: bfloat16 [256, 8192], P('req', 'kvh')
The draws below stay inside these ranges and needn't reach their ends.
Inputs may be any that keep to these rules, and one draw needn't show every extreme that they name: `history_lengths`: each request's live history rows are its first rows; some request has 512 of them in every draw.
All inputs are finite; a program needn't handle non-finite values.
Results may differ from the reference program's by a relative error of at most 0.014.
Values may be sent and summed in bfloat16 or wider, within the bound.
A program may use at most 128 MiB of HBM per device.

```python
import math
import jax
import jax.numpy as jnp
import numpy as np
from jax import lax

D = 8192
HQ = 64
KVH = 8
HD = 128
TASK_DEV = 2048
HIST = 512
HOLDERS = 2
REQUESTS = 256
CORPUS = 65536
TASKS = 8
TASK_TOKENS = 32768


def draw_queries(key, part):
    values = jnp.clip(jax.random.normal(key, (REQUESTS, HQ * HD), jnp.float32), -6.0, 6.0) * 3.0
    return values.astype(jnp.bfloat16)


def draw_history_lengths(key, part):
    lengths = jax.random.randint(key, (REQUESTS,), 1, HIST + 1, jnp.int32)
    chosen = jax.random.randint(jax.random.fold_in(key, 7), (), 0, REQUESTS, jnp.int32)
    return lengths.at[chosen].set(HIST)


def place_ends(result, stream_key, low, top_value):
    shape = result.shape
    place = [jax.random.randint(jax.random.fold_in(stream_key, axis), (), 0, shape[axis]) for axis in range(len(shape))]
    result = result.at[tuple(place)].set(low)
    longest = shape.index(max(shape))
    place[longest] = (place[longest] + 1) % shape[longest]
    return result.at[tuple(place)].set(top_value)


def level_of(key, extent, pieces, smallest, largest):
    level = 1.0
    for dim, blocks in pieces:
        steps = jax.random.uniform(jax.random.fold_in(jax.random.fold_in(key, 6), dim), (blocks,), jnp.float32, smallest / len(pieces), largest / len(pieces))
        level = level * jnp.repeat(jnp.exp(steps), extent[dim] // blocks).reshape((-1,) + (1,) * (len(extent) - 1 - dim))
    return level


def rank_table(number_of, skew):
    loads = [(1 << 20) // math.isqrt(rank ** skew) + 1 for rank in range(1, number_of + 1)]
    width = 1 + sum(loads) // (1 << 30)
    return np.cumsum(np.array([max(1, weight // width) for weight in loads]))


def ranked(own_key, dims, amount, skew):
    listing = rank_table(amount, skew)
    pick = jax.random.randint(jax.random.fold_in(own_key, 1), dims, 0, int(listing[amount - 1]))
    grade = jnp.searchsorted(jnp.asarray(listing, jnp.int32), pick, side="right")
    return jax.random.permutation(jax.random.fold_in(own_key, 2), amount)[grade].astype(jnp.int32)


def scatter_about(stream_key, shape, width, limit, cuts=(), kind=jnp.bfloat16):
    values = jax.random.normal(stream_key, shape, jnp.float32) * width
    if len(cuts) > 0:
        values = level_of(stream_key, shape, cuts, -0.22, 0.18) * values
    return jnp.clip(values, min=-limit, max=limit).astype(kind)


def setup_inputs(seed: int = 0) -> dict:
    key_of = jax.random.split(jax.random.key(seed), 11)
    queries = draw_queries(jax.random.fold_in(key_of[10], 71), 0)
    corpus_keys = scatter_about(key_of[1], (CORPUS, KVH * HD), 1.0, 6.0, ((0, 16), (1, 8)))
    corpus_values = scatter_about(key_of[2], (CORPUS, KVH * HD), 1.0, 6.0, ((0, 16), (1, 8)))
    task_keys = scatter_about(key_of[3], (TASK_TOKENS, KVH * HD), 1.15, 7.0, ((0, 16), (1, 8)))
    task_values = scatter_about(key_of[4], (TASK_TOKENS, KVH * HD), 1.0, 6.0, ((0, 16), (1, 8)))
    history_keys = scatter_about(key_of[5], (REQUESTS * HIST, KVH * HD), 1.35, 8.0, ((0, 16), (1, 8)))
    history_values = scatter_about(key_of[6], (REQUESTS * HIST, KVH * HD), 1.0, 6.0, ((0, 16), (1, 8)))
    history_lengths = draw_history_lengths(jax.random.fold_in(key_of[10], 71), 0)
    task_of = place_ends(ranked(key_of[8], (REQUESTS,), TASKS, 2), jax.random.fold_in(key_of[8], 3), 0, TASKS - 1).astype(jnp.int32)
    out_weight = scatter_about(key_of[9], (HQ * HD, D), (HQ * HD) ** -0.5, 0.0625, ((0, 8),))
    return {"queries": queries, "corpus_keys": corpus_keys, "corpus_values": corpus_values, "task_keys": task_keys, "task_values": task_values, "history_keys": history_keys, "history_values": history_values, "history_lengths": history_lengths, "task_of": task_of, "out_weight": out_weight}


def reference(queries, corpus_keys, corpus_values, task_keys, task_values, history_keys, history_values, history_lengths, task_of, out_weight):
    group = HQ // KVH
    scale = 1.0 / math.sqrt(HD)
    span = HOLDERS * TASK_DEV
    corpus_kf = corpus_keys.astype(jnp.float32).reshape(CORPUS, KVH, HD)
    corpus_vf = corpus_values.astype(jnp.float32).reshape(CORPUS, KVH, HD)
    task_kf = task_keys.astype(jnp.float32).reshape(TASK_TOKENS, KVH, HD)
    task_vf = task_values.astype(jnp.float32).reshape(TASK_TOKENS, KVH, HD)

    def rounded(weights):
        narrow = lax.optimization_barrier(weights.astype(jnp.bfloat16))
        return narrow.astype(jnp.float32)

    def single(index):
        query = lax.dynamic_slice_in_dim(queries, index, 1, 0).astype(jnp.float32).reshape(KVH, group, HD)
        start = (task_of[index] * span).astype(jnp.int32)
        tkeys = lax.dynamic_slice_in_dim(task_kf, start, span, 0)
        tvals = lax.dynamic_slice_in_dim(task_vf, start, span, 0)
        hstart = (index * HIST).astype(jnp.int32)
        hkeys = lax.dynamic_slice_in_dim(history_keys, hstart, HIST, 0).astype(jnp.float32).reshape(HIST, KVH, HD)
        hvals = lax.dynamic_slice_in_dim(history_values, hstart, HIST, 0).astype(jnp.float32).reshape(HIST, KVH, HD)
        first = jnp.einsum('kgd,skd->kgs', query, corpus_kf) * scale
        second = jnp.einsum('kgd,skd->kgs', query, tkeys) * scale
        third = jnp.einsum('kgd,skd->kgs', query, hkeys) * scale
        valid = jnp.arange(HIST, dtype=jnp.int32) < history_lengths[index]
        third = jnp.where(valid, third, -jnp.inf)
        top = jnp.maximum(jnp.maximum(lax.optimization_barrier(jnp.max(first, -1)), lax.optimization_barrier(jnp.max(second, -1))), lax.optimization_barrier(jnp.max(third, -1)))
        pone = jnp.exp(first - top[..., None])
        ptwo = jnp.exp(second - top[..., None])
        pthree = jnp.where(valid, jnp.exp(third - top[..., None]), 0.0)
        total = lax.optimization_barrier(jnp.sum(pone, -1)) + lax.optimization_barrier(jnp.sum(ptwo, -1)) + lax.optimization_barrier(jnp.sum(pthree, -1))
        summed = jnp.einsum('kgs,skd->kgd', rounded(pone), corpus_vf)
        summed = summed + jnp.einsum('kgs,skd->kgd', rounded(ptwo), tvals)
        summed = summed + jnp.einsum('kgs,skd->kgd', rounded(pthree), hvals)
        return (summed / total[..., None]).reshape(HQ * HD).astype(jnp.bfloat16)
    attended = lax.map(single, jnp.arange(REQUESTS, dtype=jnp.int32))
    return jnp.dot(attended, out_weight, preferred_element_type=jnp.float32).astype(jnp.bfloat16)
```

```python
import functools
import math

import jax
import jax.numpy as jnp
from jax import lax
from jax.experimental import pallas as pl
from jax.experimental.pallas import tpu as pltpu
from jax.sharding import PartitionSpec as P

HD = 128
HOLDERS = 2
MESH = pl.DeviceIdType.MESH
F32 = jnp.float32
BF16 = jnp.bfloat16
CS = math.log2(math.e) / math.sqrt(HD)
FAR = 1e30
NT = (((1,), (1,)), ((), ()))
TN = (((0,), (0,)), ((), ()))


def ring4(a):
    return a + a // 2 - 2 * (a // 3)


def kernel(
    q_hbm,
    ck_hbm,
    cv_hbm,
    tk_hbm,
    tv_hbm,
    hk_hbm,
    hv_hbm,
    len_ref,
    task_ref,
    w_hbm,
    out_ref,
    q_all,
    kbuf,
    vbuf,
    vt,
    hkb,
    hvb,
    wbuf,
    sa,
    sb,
    osend,
    orecv,
    hs,
    hq,
    hot,
    hlse,
    valid,
    psend,
    precv,
    ld_sem,
    q_send,
    q_recv,
    o_send,
    o_recv,
    p_send,
    p_recv,
):
    nreq, rows, width = q_all.shape
    nkv = psend.shape[0]
    heads = width // HD
    cols = rows * heads
    corpus = ck_hbm.shape[0]
    keys = kbuf.shape[0]
    hist = hkb.shape[0] // rows
    out_w = psend.shape[2]
    chunk = 512
    nch, ncorp = keys // chunk, corpus // chunk
    me = lax.axis_index("req")
    mj = lax.axis_index("kvh")
    y, x = me // 4, me % 4
    mz, mc = mj // 2, mj % 2

    def peer(k, sign):
        dy, dx = ring4(k // 4), ring4(k % 4)
        return ((y + 4 + sign * dy) % 4) * 4 + (x + 4 + sign * dx) % 4

    def kv_peer(e, sign):
        dz, dc = ring4(e // 2), e % 2
        return ((mz + 4 + sign * dz) % 4) * 2 + (mc + dc) % 2

    loads = [
        pltpu.make_async_copy(q_hbm, q_all.at[0], ld_sem.at[0]),
        pltpu.make_async_copy(hk_hbm, hkb, ld_sem.at[1]),
        pltpu.make_async_copy(hv_hbm, hvb, ld_sem.at[2]),
        pltpu.make_async_copy(cv_hbm, vbuf.at[pl.ds(0, corpus)], ld_sem.at[3]),
        pltpu.make_async_copy(tv_hbm, vbuf.at[pl.ds(corpus, keys - corpus)], ld_sem.at[4]),
        pltpu.make_async_copy(ck_hbm, kbuf.at[pl.ds(0, corpus)], ld_sem.at[5]),
        pltpu.make_async_copy(tk_hbm, kbuf.at[pl.ds(corpus, keys - corpus)], ld_sem.at[6]),
        pltpu.make_async_copy(w_hbm, wbuf, ld_sem.at[7]),
    ]
    for c in loads:
        c.start()

    barrier = pltpu.get_barrier_semaphore()

    def greet_req(k, carry):
        pl.semaphore_signal(barrier, inc=1, device_id={"req": peer(k, 1)}, device_id_type=MESH)
        return carry

    def greet_kv(e, carry):
        pl.semaphore_signal(barrier, inc=1, device_id={"kvh": kv_peer(e, 1)}, device_id_type=MESH)
        return carry

    lax.fori_loop(1, nreq, greet_req, 0)
    lax.fori_loop(1, nkv, greet_kv, 0)
    pl.semaphore_wait(barrier, nreq + nkv - 2)

    loads[0].wait()

    def q_copy(k):
        return pltpu.make_async_remote_copy(
            src_ref=q_all.at[0],
            dst_ref=q_all.at[k],
            send_sem=q_send.at[k],
            recv_sem=q_recv.at[k],
            device_id={"req": peer(k, -1)},
            device_id_type=MESH,
        )

    def send_q(k, carry):
        q_copy(k).start()
        return carry

    lax.fori_loop(1, nreq, send_q, 0)

    def head_major(k):
        block = q_all[k]
        return [block[:, h * HD : (h + 1) * HD] for h in range(heads)]

    lane = lax.broadcasted_iota(jnp.int32, (nreq, nreq * rows), 1)
    row = lax.broadcasted_iota(jnp.int32, (nreq, nreq * rows), 0)
    mine = jnp.broadcast_to(task_ref[...], lane.shape) == me // HOLDERS
    mine = jnp.where(mine & (lane // rows == row), 1.0, 0.0).astype(BF16)
    er = lax.broadcasted_iota(jnp.int32, (nreq * rows, cols), 0)
    ec = lax.broadcasted_iota(jnp.int32, (nreq * rows, cols), 1)
    spread = jnp.where(er % rows == ec % rows, 1.0, 0.0).astype(BF16)
    valid[...] = jnp.dot(mine, spread, preferred_element_type=F32)

    pr = lax.broadcasted_iota(jnp.int32, (cols, cols), 0)
    pc = lax.broadcasted_iota(jnp.int32, (cols, cols), 1)
    perm = jnp.where((pr % heads == pc // rows) & (pr // heads == pc % rows), 1.0, 0.0)
    perm16 = perm.astype(BF16)
    hq[...] = jnp.dot(perm16, jnp.concatenate(head_major(0), 0), preferred_element_type=F32)
    loads[1].wait()
    hcol = lax.broadcasted_iota(jnp.int32, (heads, hist), 1)
    for r in range(rows):
        at = slice(r * heads, (r + 1) * heads)
        s = lax.dot_general(
            hq[at, :].astype(BF16),
            hkb[r * hist : (r + 1) * hist, :],
            NT,
            preferred_element_type=F32,
        )
        hs[at, :] = jnp.where(hcol < len_ref[r], s, -FAR)
    s = hs[...]
    hm = jnp.max(s, axis=1, keepdims=True)
    p = jnp.exp2((s - hm) * CS)
    htot = jnp.sum(p, axis=1, keepdims=True)
    hs[...] = p
    loads[2].wait()
    for r in range(rows):
        at = slice(r * heads, (r + 1) * heads)
        hq[at, :] = jnp.dot(
            hs[at, :].astype(BF16), hvb[r * hist : (r + 1) * hist, :], preferred_element_type=F32
        )
    ho = (hq[...] * (1.0 / htot)).astype(BF16)
    hot[...] = lax.dot_general(ho, perm16, TN, preferred_element_type=F32)
    hl = jnp.sum(perm * (hm * CS + jnp.log2(htot)), axis=0, keepdims=True)
    hlse[...] = jnp.broadcast_to(hl, hlse.shape)

    loads[3].wait()
    loads[4].wait()
    for c in range(nch):
        at = slice(c * chunk, (c + 1) * chunk)
        vt[:HD, at] = vbuf[at, :].T
    vt[HD:, :] = jnp.ones((vt.shape[0] - HD, keys), BF16)
    loads[5].wait()
    loads[6].wait()

    def arrive(b):
        for a in range(2):
            k = 2 * b + a
            if isinstance(b, int) and k == 0:
                continue
            q_copy(k).wait_recv()

    def q_block(b):
        return jnp.concatenate(head_major(2 * b) + head_major(2 * b + 1), 0)

    def score(c, q, sref, peaks):
        at = slice(c * chunk, (c + 1) * chunk)
        s = lax.dot_general(kbuf[at, :], q, NT, preferred_element_type=F32)
        sref[at, :] = s
        part = jnp.max(s.reshape(chunk // 8, 8, 2 * cols), axis=0)
        g = 0 if c < ncorp else 1
        peaks[g] = part if peaks[g] is None else jnp.maximum(peaks[g], part)

    def weigh(c, sref, shifts, acc):
        at = slice(c * chunk, (c + 1) * chunk)
        p = jnp.exp2(sref[at, :] * CS - shifts[0 if c < ncorp else 1]).astype(BF16)
        part = jnp.dot(vt[:, at], p, preferred_element_type=F32)
        return part if acc is None else acc + part

    def o_copy(k):
        return pltpu.make_async_remote_copy(
            src_ref=osend.at[k],
            dst_ref=orecv.at[k],
            send_sem=o_send.at[k],
            recv_sem=o_recv.at[k],
            device_id={"req": peer(k, 1)},
            device_id_type=MESH,
        )

    def stage(b, s_now, s_next, peaks):
        mask = jnp.concatenate([valid[pl.ds(peer(2 * b + a, 1), 1), :] for a in range(2)], 1) > 0
        pk = [jnp.max(m, axis=0, keepdims=True) for m in peaks]
        top = jnp.maximum(pk[0], jnp.where(mask, pk[1], -FAR)) * CS
        shifts = [top, jnp.where(mask, top, FAR)]
        later = [None, None]
        if s_next is not None:
            arrive(b + 1)
            q = q_block(b + 1)
        acc = None
        for c in range(nch):
            if s_next is not None:
                score(c, q, s_next, later)
            acc = weigh(c, s_now, shifts, acc)
        total = acc[HD : HD + 1, :]
        o = (acc[:HD, :] * (1.0 / total)).astype(BF16)
        lse = top + jnp.log2(total)
        hi = lse.astype(BF16).astype(F32)
        mid = (lse - hi).astype(BF16).astype(F32)
        lo = lse - hi - mid
        sub = lax.broadcasted_iota(jnp.int32, (16, 2 * cols), 0)
        info = jnp.where(sub == 0, hi, jnp.where(sub == 1, mid, jnp.where(sub == 2, lo, 0.0)))
        info = info.astype(BF16)
        for a in range(2):
            k = 2 * b + a
            at = slice(a * cols, (a + 1) * cols)
            osend[k, :HD, :] = o[:, at]
            osend[k, HD:, :] = info[:, at]
            if isinstance(k, int):
                if k > 0:
                    o_copy(k).start()
            else:
                pl.when(k > 0)(lambda k=k: o_copy(k).start())
        return later

    arrive(0)
    peaks = [None, None]
    q0 = q_block(0)
    for c in range(nch):
        score(c, q0, sa, peaks)

    def pair(i, peaks):
        peaks = stage(2 * i, sa, sb, list(peaks))
        peaks = stage(2 * i + 1, sb, sa, peaks)
        return tuple(peaks)

    nb = nreq // 2
    peaks = list(lax.fori_loop(0, nb // 2 - 1, pair, tuple(peaks)))
    peaks = stage(nb - 2, sa, sb, peaks)
    stage(nb - 1, sb, None, peaks)

    def arrived(k, carry):
        o_copy(k).wait_recv()
        return carry

    lax.fori_loop(1, nreq, arrived, 0)

    def part(k):
        return osend if k == 0 else orecv

    lses = [
        jnp.sum(part(k)[k, HD:, :].astype(F32), axis=0, keepdims=True) for k in range(nreq)
    ]
    lses.append(hlse[0:1, :])
    top = functools.reduce(jnp.maximum, lses)
    ws = [jnp.exp2(v - top) for v in lses]
    den = functools.reduce(jnp.add, ws)
    att = hot[...] * ws[nreq]
    for k in range(nreq):
        att = att + part(k)[k, :HD, :].astype(F32) * ws[k]
    att = (att * (1.0 / den)).T.astype(BF16)
    att = jnp.concatenate([att[h * rows : (h + 1) * rows, :] for h in range(heads)], 1)

    loads[7].wait()

    def p_copy(e):
        return pltpu.make_async_remote_copy(
            src_ref=psend.at[e],
            dst_ref=precv.at[e],
            send_sem=p_send.at[e],
            recv_sem=p_recv.at[e],
            device_id={"kvh": kv_peer(e, 1)},
            device_id_type=MESH,
        )

    def project(e):
        at = pl.ds(pl.multiple_of(kv_peer(e, 1) * out_w, out_w), out_w)
        return jnp.dot(att, wbuf[:, at], preferred_element_type=F32)

    def send_p(t, carry):
        e = nkv - 1 - t
        psend[e] = project(e).astype(BF16)
        p_copy(e).start()
        return carry

    lax.fori_loop(0, nkv - 1, send_p, 0)
    mixed = project(0)
    for e in range(1, nkv):
        p_copy(e).wait_recv()
        mixed = mixed + precv[e].astype(F32)
    out_ref[...] = mixed.astype(BF16)

    def sent(k, carry):
        q_copy(k).wait_send()
        o_copy(k).wait_send()
        return carry

    lax.fori_loop(1, nreq, sent, 0)

    def p_sent(e, carry):
        p_copy(e).wait_send()
        return carry

    lax.fori_loop(1, nkv, p_sent, 0)


def solution(mesh):
    nreq, nkv = mesh.shape["req"], mesh.shape["kvh"]

    def shards(q, ck, cv, tk, tv, hk, hv, lengths, task_of, w):
        rows, width = q.shape
        cols = rows * (width // HD)
        keys = ck.shape[0] + tk.shape[0]
        hist = hk.shape[0] // rows
        out_w = w.shape[1] // nkv
        hbm = pl.BlockSpec(memory_space=pl.ANY)
        vmem = pl.BlockSpec(memory_space=pltpu.VMEM)
        smem = pl.BlockSpec(memory_space=pltpu.SMEM)
        dma = pltpu.SemaphoreType.DMA
        return pl.pallas_call(
            kernel,
            out_shape=jax.ShapeDtypeStruct((rows, out_w), BF16),
            in_specs=[hbm] * 7 + [smem, vmem, hbm],
            out_specs=vmem,
            scratch_shapes=[
                pltpu.VMEM((nreq, rows, width), BF16),
                pltpu.VMEM((keys, HD), BF16),
                pltpu.VMEM((keys, HD), BF16),
                pltpu.VMEM((HD + 16, keys), BF16),
                pltpu.VMEM(hk.shape, BF16),
                pltpu.VMEM(hv.shape, BF16),
                pltpu.VMEM(w.shape, BF16),
                pltpu.VMEM((keys, 2 * cols), F32),
                pltpu.VMEM((keys, 2 * cols), F32),
                pltpu.VMEM((nreq, HD + 16, cols), BF16),
                pltpu.VMEM((nreq, HD + 16, cols), BF16),
                pltpu.VMEM((cols, hist), F32),
                pltpu.VMEM((cols, HD), F32),
                pltpu.VMEM((HD, cols), F32),
                pltpu.VMEM((8, cols), F32),
                pltpu.VMEM((nreq, cols), F32),
                pltpu.VMEM((nkv, rows, out_w), BF16),
                pltpu.VMEM((nkv, rows, out_w), BF16),
                dma((8,)),
                dma((nreq,)),
                dma((nreq,)),
                dma((nreq,)),
                dma((nreq,)),
                dma((nkv,)),
                dma((nkv,)),
            ],
            compiler_params=pltpu.CompilerParams(
                collective_id=0, has_side_effects=True, vmem_limit_bytes=60 * 2**20
            ),
        )(q, ck, cv, tk, tv, hk, hv, lengths, task_of.reshape(1, -1), w)

    return jax.shard_map(
        shards,
        mesh=mesh,
        in_specs=(P("req", "kvh"),) * 7 + (P("req"), P(), P("kvh", None)),
        out_specs=P("req", "kvh"),
        check_vma=False,
    )
```

```python
import functools
import math

import jax
import jax.numpy as jnp
from jax import lax
from jax.experimental import pallas as pl
from jax.experimental.pallas import tpu as pltpu
from jax.sharding import PartitionSpec as P

HD = 128
HOLDERS = 2
MESH = pl.DeviceIdType.MESH
F32 = jnp.float32
BF16 = jnp.bfloat16
CS = math.log2(math.e) / math.sqrt(HD)
FAR = 1e30
NT = (((1,), (1,)), ((), ()))
TN = (((0,), (0,)), ((), ()))


def kernel(
    q_hbm,
    ck_hbm,
    cv_hbm,
    tk_hbm,
    tv_hbm,
    hk_hbm,
    hv_hbm,
    len_hbm,
    task_hbm,
    w_hbm,
    out_ref,
    q_all,
    kbuf,
    vbuf,
    vt,
    hkb,
    hvb,
    len_ref,
    task_ref,
    wbuf,
    sa,
    sb,
    pa,
    pb,
    osend,
    orecv,
    xsend,
    xrecv,
    hs,
    hq,
    hot,
    hlse,
    valid,
    psib,
    prib,
    psend,
    precv,
    ld_sem,
    q_send,
    q_recv,
    o_send,
    o_recv,
    x_send,
    x_recv,
    b_send,
    b_recv,
    p_send,
    p_recv,
):
    nreq, rows, width = q_all.shape
    heads = width // HD
    cols = rows * heads
    corpus = ck_hbm.shape[0]
    keys = kbuf.shape[0]
    hist = hkb.shape[0] // rows
    out_w = psend.shape[2]
    chunk, deep = 512, 2048
    nch, ncorp, per = keys // chunk, corpus // chunk, deep // chunk
    me = lax.axis_index("req")
    mj = lax.axis_index("kvh")
    y, x = me // 4, me % 4
    mz, mc = mj // 2, mj % 2

    def off(t):
        dy = 3 - t // 4
        return dy, (t % 4 + 1 + dy) % 4

    def slot(t):
        dy, dx = off(t)
        return dy * 4 + dx

    def peer(t, sign):
        dy, dx = off(t)
        return ((y + 4 + sign * dy) % 4) * 4 + (x + 4 + sign * dx) % 4

    def greet(**device):
        pl.semaphore_signal(
            pltpu.get_barrier_semaphore(), inc=1, device_id=device, device_id_type=MESH
        )

    def greet_req(t, carry):
        greet(req=peer(t, -1))
        return carry

    lax.fori_loop(0, nreq - 1, greet_req, 0)
    greet(kvh=mz * 2 + 1 - mc)
    for dz in range(1, 4):
        greet(kvh=((mz + dz) % 4) * 2 + mc)

    loads = [
        pltpu.make_async_copy(q_hbm, q_all.at[0], ld_sem.at[0]),
        pltpu.make_async_copy(task_hbm, task_ref, ld_sem.at[1]),
        pltpu.make_async_copy(len_hbm, len_ref, ld_sem.at[2]),
        pltpu.make_async_copy(cv_hbm, vbuf.at[pl.ds(0, corpus)], ld_sem.at[3]),
        pltpu.make_async_copy(tv_hbm, vbuf.at[pl.ds(corpus, keys - corpus)], ld_sem.at[4]),
        pltpu.make_async_copy(hk_hbm, hkb, ld_sem.at[5]),
        pltpu.make_async_copy(hv_hbm, hvb, ld_sem.at[6]),
        pltpu.make_async_copy(ck_hbm, kbuf.at[pl.ds(0, corpus)], ld_sem.at[7]),
        pltpu.make_async_copy(tk_hbm, kbuf.at[pl.ds(corpus, keys - corpus)], ld_sem.at[8]),
        pltpu.make_async_copy(w_hbm, wbuf, ld_sem.at[9]),
    ]
    for c in loads:
        c.start()

    loads[1].wait()
    lane = lax.broadcasted_iota(jnp.int32, (nreq, nreq * rows), 1)
    row = lax.broadcasted_iota(jnp.int32, (nreq, nreq * rows), 0)
    mine = jnp.broadcast_to(task_ref[...], lane.shape) == me // HOLDERS
    mine = jnp.where(mine & (lane // rows == row), 1.0, 0.0).astype(BF16)
    er = lax.broadcasted_iota(jnp.int32, (nreq * rows, cols), 0)
    ec = lax.broadcasted_iota(jnp.int32, (nreq * rows, cols), 1)
    spread = jnp.where(er % rows == ec % rows, 1.0, 0.0).astype(BF16)
    valid[...] = jnp.dot(mine, spread, preferred_element_type=F32)

    loads[0].wait()
    pl.semaphore_wait(pltpu.get_barrier_semaphore(), nreq - 1 + 4)

    def q_copy(t):
        return pltpu.make_async_remote_copy(
            src_ref=q_all.at[0],
            dst_ref=q_all.at[slot(t)],
            send_sem=q_send.at[t],
            recv_sem=q_recv.at[t],
            device_id={"req": peer(t, -1)},
            device_id_type=MESH,
        )

    def send_q(t, carry):
        q_copy(t).start()
        return carry

    lax.fori_loop(0, nreq - 1, send_q, 0)

    def head_major(k):
        block = q_all[k]
        return [block[:, h * HD : (h + 1) * HD] for h in range(heads)]

    loads[3].wait()
    loads[4].wait()
    for c in range(nch):
        at = slice(c * chunk, (c + 1) * chunk)
        vt[:HD, at] = vbuf[at, :].T
    vt[HD:, :] = jnp.ones((vt.shape[0] - HD, keys), BF16)

    pr = lax.broadcasted_iota(jnp.int32, (cols, cols), 0)
    pc = lax.broadcasted_iota(jnp.int32, (cols, cols), 1)
    perm = jnp.where((pr % heads == pc // rows) & (pr // heads == pc % rows), 1.0, 0.0)
    perm16 = perm.astype(BF16)
    hq[...] = jnp.dot(perm16, jnp.concatenate(head_major(0), 0), preferred_element_type=F32)
    loads[2].wait()
    loads[5].wait()
    hcol = lax.broadcasted_iota(jnp.int32, (heads, hist), 1)
    for r in range(rows):
        at = slice(r * heads, (r + 1) * heads)
        s = lax.dot_general(
            hq[at, :].astype(BF16),
            hkb[r * hist : (r + 1) * hist, :],
            NT,
            preferred_element_type=F32,
        )
        hs[at, :] = jnp.where(hcol < len_ref[r], s, -FAR)
    s = hs[...]
    hm = jnp.max(s, axis=1, keepdims=True)
    p = jnp.exp2((s - hm) * CS)
    htot = jnp.sum(p, axis=1, keepdims=True)
    hs[...] = p
    loads[6].wait()
    for r in range(rows):
        at = slice(r * heads, (r + 1) * heads)
        hq[at, :] = jnp.dot(
            hs[at, :].astype(BF16), hvb[r * hist : (r + 1) * hist, :], preferred_element_type=F32
        )
    ho = (hq[...] * (1.0 / htot)).astype(BF16)
    hot[...] = lax.dot_general(ho, perm16, TN, preferred_element_type=F32)
    hl = jnp.sum(perm * (hm * CS + jnp.log2(htot)), axis=0, keepdims=True)
    hlse[...] = jnp.broadcast_to(hl, hlse.shape)
    loads[7].wait()
    loads[8].wait()

    def arrive(b):
        for a in range(2):
            t = 2 * b + a
            if isinstance(t, int) and t == nreq - 1:
                continue
            q_copy(t).wait_recv()

    def q_pair(b):
        return jnp.concatenate(head_major(slot(2 * b)) + head_major(slot(2 * b + 1)), 0)

    def score(c, q, sref, peaks):
        at = slice(c * chunk, (c + 1) * chunk)
        s = lax.dot_general(kbuf[at, :], q, NT, preferred_element_type=F32)
        sref[at, :] = s
        part = jnp.max(s.reshape(chunk // 8, 8, 2 * cols), axis=0)
        g = 0 if c < ncorp else 1
        peaks[g] = part if peaks[g] is None else jnp.maximum(peaks[g], part)

    def weigh(c, sref, pref, shifts):
        at = slice(c * chunk, (c + 1) * chunk)
        p = jnp.exp2(sref[at, :] * CS - shifts[0 if c < ncorp else 1])
        pref[at, :] = p.astype(BF16)

    def add_up(g, pref, acc):
        at = slice(g * deep, (g + 1) * deep)
        part = jnp.dot(vt[:, at], pref[at, :], preferred_element_type=F32)
        return part if acc is None else acc + part

    def y_copy(t):
        dy, dx = off(t)
        return pltpu.make_async_remote_copy(
            src_ref=osend.at[slot(t)],
            dst_ref=orecv.at[slot(t)],
            send_sem=o_send.at[t],
            recv_sem=o_recv.at[t],
            device_id={"req": ((y + dy) % 4) * 4 + x},
            device_id_type=MESH,
        )

    def pack(lse):
        hi = lse.astype(BF16).astype(F32)
        mid = (lse - hi).astype(BF16).astype(F32)
        lo = lse - hi - mid
        sub = lax.broadcasted_iota(jnp.int32, (16, lse.shape[1]), 0)
        info = jnp.where(sub == 0, hi, jnp.where(sub == 1, mid, jnp.where(sub == 2, lo, 0.0)))
        return info.astype(BF16)

    def unpack(ref, k):
        lse = jnp.sum(ref[k, HD:, :].astype(F32), axis=0, keepdims=True)
        return ref[k, :HD, :].astype(F32), lse

    def merge(parts):
        top = functools.reduce(jnp.maximum, [v for _, v in parts])
        ws = [jnp.exp2(v - top) for _, v in parts]
        den = functools.reduce(jnp.add, ws)
        inv = 1.0 / den
        o = functools.reduce(jnp.add, [o * (w * inv) for (o, _), w in zip(parts, ws)])
        return o, top + jnp.log2(den)

    def stage(b, s_now, s_next, pref, peaks):
        mask = jnp.concatenate([valid[pl.ds(peer(2 * b + a, 1), 1), :] for a in range(2)], 1) > 0
        pk = [jnp.max(m, axis=0, keepdims=True) for m in peaks]
        top = jnp.maximum(pk[0], jnp.where(mask, pk[1], -FAR)) * CS
        shifts = [top, jnp.where(mask, top, FAR)]
        later = [None, None]
        if s_next is not None:
            arrive(b + 1)
            q = q_pair(b + 1)
        acc, done = None, 0
        for c in range(nch):
            if s_next is not None:
                score(c, q, s_next, later)
            weigh(c, s_now, pref, shifts)
            if (done + 1) * per <= c:
                acc = add_up(done, pref, acc)
                done += 1
        while done * deep < keys:
            acc = add_up(done, pref, acc)
            done += 1
        total = acc[HD : HD + 1, :]
        o = (acc[:HD, :] * (1.0 / total)).astype(BF16)
        info = pack(top + jnp.log2(total))
        for a in range(2):
            t = 2 * b + a
            at = slice(a * cols, (a + 1) * cols)
            osend[slot(t), :HD, :] = o[:, at]
            osend[slot(t), HD:, :] = info[:, at]
            if not isinstance(t, int) or t < nreq - 4:
                y_copy(t).start()
        return later

    arrive(0)
    peaks = [None, None]
    q0 = q_pair(0)
    for c in range(nch):
        score(c, q0, sa, peaks)

    def twice(i, peaks):
        peaks = stage(2 * i, sa, sb, pa, list(peaks))
        peaks = stage(2 * i + 1, sb, sa, pb, peaks)
        return tuple(peaks)

    nb = nreq // 2
    peaks = list(lax.fori_loop(0, nb // 2 - 1, twice, tuple(peaks)))
    peaks = stage(nb - 2, sa, sb, pa, peaks)
    stage(nb - 1, sb, None, pb, peaks)

    def y_arrived(t, carry):
        y_copy(t).wait_recv()
        return carry

    lax.fori_loop(0, nreq - 4, y_arrived, 0)

    def x_copy(dx):
        return pltpu.make_async_remote_copy(
            src_ref=xsend.at[dx],
            dst_ref=xrecv.at[dx],
            send_sem=x_send.at[dx],
            recv_sem=x_recv.at[dx],
            device_id={"req": y * 4 + (x + dx) % 4},
            device_id_type=MESH,
        )

    def along_y(dx):
        return merge([unpack(osend, dx)] + [unpack(orecv, dy * 4 + dx) for dy in range(1, 4)])

    for dx in (2, 1, 3):
        o, lse = along_y(dx)
        xsend[dx, :HD, :] = o.astype(BF16)
        xsend[dx, HD:, :] = pack(lse)
        x_copy(dx).start()
    home = merge([along_y(0), (hot[...], hlse[0:1, :])])
    for dx in (1, 3, 2):
        x_copy(dx).wait_recv()
    att, _ = merge([home] + [unpack(xrecv, dx) for dx in range(1, 4)])
    att = att.T.astype(BF16)
    att = jnp.concatenate([att[h * rows : (h + 1) * rows, :] for h in range(heads)], 1)

    loads[9].wait()

    def project(z, c):
        at = pl.ds(pl.multiple_of((z * 2 + c) * out_w, out_w), out_w)
        return jnp.dot(att, wbuf[:, at], preferred_element_type=F32)

    def b_copy(dz):
        return pltpu.make_async_remote_copy(
            src_ref=psib.at[dz],
            dst_ref=prib.at[dz],
            send_sem=b_send.at[dz],
            recv_sem=b_recv.at[dz],
            device_id={"kvh": mz * 2 + 1 - mc},
            device_id_type=MESH,
        )

    def p_copy(dz):
        return pltpu.make_async_remote_copy(
            src_ref=psend.at[dz],
            dst_ref=precv.at[dz],
            send_sem=p_send.at[dz],
            recv_sem=p_recv.at[dz],
            device_id={"kvh": ((mz + dz) % 4) * 2 + mc},
            device_id_type=MESH,
        )

    def give(i, carry):
        dz = (2 + i) % 4
        psib[dz] = project((mz + dz) % 4, 1 - mc).astype(BF16)
        b_copy(dz).start()
        return carry

    lax.fori_loop(0, 4, give, 0)

    def both(dz):
        own = project((mz + dz) % 4, mc)
        b_copy(dz).wait_recv()
        return own + prib[dz].astype(F32)

    def forward(i, carry):
        dz = 2 + i - 3 * (i // 2)
        psend[dz] = both(dz).astype(BF16)
        p_copy(dz).start()
        return carry

    lax.fori_loop(0, 3, forward, 0)
    mixed = both(0)
    for dz in (3, 1, 2):
        p_copy(dz).wait_recv()
        mixed = mixed + precv[dz].astype(F32)
    out_ref[...] = mixed.astype(BF16)

    def q_sent(t, carry):
        q_copy(t).wait_send()
        return carry

    lax.fori_loop(0, nreq - 1, q_sent, 0)

    def y_sent(t, carry):
        y_copy(t).wait_send()
        return carry

    lax.fori_loop(0, nreq - 4, y_sent, 0)
    for d in range(1, 4):
        x_copy(d).wait_send()
        p_copy(d).wait_send()
    for d in range(4):
        b_copy(d).wait_send()


def solution(mesh):
    nreq, nkv = mesh.shape["req"], mesh.shape["kvh"]

    def shards(q, ck, cv, tk, tv, hk, hv, lengths, task_of, w):
        rows, width = q.shape
        cols = rows * (width // HD)
        keys = ck.shape[0] + tk.shape[0]
        hist = hk.shape[0] // rows
        out_w = w.shape[1] // nkv
        hbm = pl.BlockSpec(memory_space=pl.ANY)
        vmem = pl.BlockSpec(memory_space=pltpu.VMEM)
        dma = pltpu.SemaphoreType.DMA
        return pl.pallas_call(
            kernel,
            out_shape=jax.ShapeDtypeStruct((rows, out_w), BF16),
            in_specs=[hbm] * 10,
            out_specs=vmem,
            scratch_shapes=[
                pltpu.VMEM((nreq, rows, width), BF16),
                pltpu.VMEM((keys, HD), BF16),
                pltpu.VMEM((keys, HD), BF16),
                pltpu.VMEM((HD + 16, keys), BF16),
                pltpu.VMEM(hk.shape, BF16),
                pltpu.VMEM(hv.shape, BF16),
                pltpu.SMEM(lengths.shape, jnp.int32),
                pltpu.VMEM((1, nreq * rows), jnp.int32),
                pltpu.VMEM(w.shape, BF16),
                pltpu.VMEM((keys, 2 * cols), F32),
                pltpu.VMEM((keys, 2 * cols), F32),
                pltpu.VMEM((keys, 2 * cols), BF16),
                pltpu.VMEM((keys, 2 * cols), BF16),
                pltpu.VMEM((nreq, HD + 16, cols), BF16),
                pltpu.VMEM((nreq, HD + 16, cols), BF16),
                pltpu.VMEM((4, HD + 16, cols), BF16),
                pltpu.VMEM((4, HD + 16, cols), BF16),
                pltpu.VMEM((cols, hist), F32),
                pltpu.VMEM((cols, HD), F32),
                pltpu.VMEM((HD, cols), F32),
                pltpu.VMEM((8, cols), F32),
                pltpu.VMEM((nreq, cols), F32),
                pltpu.VMEM((4, rows, out_w), BF16),
                pltpu.VMEM((4, rows, out_w), BF16),
                pltpu.VMEM((4, rows, out_w), BF16),
                pltpu.VMEM((4, rows, out_w), BF16),
                dma((10,)),
                dma((nreq,)),
                dma((nreq,)),
                dma((nreq,)),
                dma((nreq,)),
                dma((4,)),
                dma((4,)),
                dma((4,)),
                dma((4,)),
                dma((4,)),
                dma((4,)),
            ],
            compiler_params=pltpu.CompilerParams(
                collective_id=0, has_side_effects=True, vmem_limit_bytes=60 * 2**20
            ),
        )(q, ck, cv, tk, tv, hk, hv, lengths, task_of.reshape(1, -1), w)

    return jax.shard_map(
        shards,
        mesh=mesh,
        in_specs=(P("req", "kvh"),) * 7 + (P("req"), P(), P("kvh", None)),
        out_specs=P("req", "kvh"),
        check_vma=False,
    )
```

```python
import functools
import math

import jax
import jax.numpy as jnp
from jax import lax
from jax.experimental import pallas as pl
from jax.experimental.pallas import tpu as pltpu
from jax.sharding import PartitionSpec as P

HD = 128
HOLDERS = 2
MESH = pl.DeviceIdType.MESH
F32 = jnp.float32
BF16 = jnp.bfloat16
CS = math.log2(math.e) / math.sqrt(HD)
FAR = 1e30
NT = (((1,), (1,)), ((), ()))
TN = (((0,), (0,)), ((), ()))


def kernel(
    q_hbm,
    ck_hbm,
    cv_hbm,
    tk_hbm,
    tv_hbm,
    hk_hbm,
    hv_hbm,
    len_hbm,
    task_hbm,
    w_hbm,
    out_ref,
    q_all,
    kbuf,
    vbuf,
    vt,
    hkb,
    hvb,
    len_ref,
    task_ref,
    wbuf,
    sa,
    sb,
    pa,
    pb,
    osend,
    orecv,
    hs,
    hq,
    valid,
    psend,
    precv,
    ld_sem,
    q_send,
    q_recv,
    o_send,
    o_recv,
    p_send,
    p_recv,
):
    nreq, rows, width = q_all.shape
    nkv = psend.shape[0]
    heads = width // HD
    cols = rows * heads
    corpus = ck_hbm.shape[0]
    keys = kbuf.shape[0]
    hist = hkb.shape[0] // rows
    out_w = psend.shape[2]
    chunk, deep = 512, 2048
    nch, ncorp, per = keys // chunk, corpus // chunk, deep // chunk
    me = lax.axis_index("req")
    mj = lax.axis_index("kvh")
    y, x = me // 4, me % 4
    mz, mc = mj // 2, mj % 2

    def off(t):
        dy = 3 - t // 4
        return dy, (t % 4 + 1 + dy) % 4

    def slot(t):
        dy, dx = off(t)
        return dy * 4 + dx

    def peer(t, sign):
        dy, dx = off(t)
        return ((y + 4 + sign * dy) % 4) * 4 + (x + 4 + sign * dx) % 4

    def greet(**device):
        pl.semaphore_signal(
            pltpu.get_barrier_semaphore(), inc=1, device_id=device, device_id_type=MESH
        )

    def greet_req(t, carry):
        greet(req=peer(t, -1))
        return carry

    lax.fori_loop(0, nreq - 1, greet_req, 0)

    def greet_kv(e, carry):
        greet(kvh=(mj + e) % nkv)
        return carry

    lax.fori_loop(1, nkv, greet_kv, 0)

    loads = [
        pltpu.make_async_copy(q_hbm, q_all.at[0], ld_sem.at[0]),
        pltpu.make_async_copy(task_hbm, task_ref, ld_sem.at[1]),
        pltpu.make_async_copy(len_hbm, len_ref, ld_sem.at[2]),
        pltpu.make_async_copy(cv_hbm, vbuf.at[pl.ds(0, corpus)], ld_sem.at[3]),
        pltpu.make_async_copy(tv_hbm, vbuf.at[pl.ds(corpus, keys - corpus)], ld_sem.at[4]),
        pltpu.make_async_copy(ck_hbm, kbuf.at[pl.ds(0, corpus)], ld_sem.at[5]),
        pltpu.make_async_copy(tk_hbm, kbuf.at[pl.ds(corpus, keys - corpus)], ld_sem.at[6]),
        pltpu.make_async_copy(hk_hbm, hkb, ld_sem.at[7]),
        pltpu.make_async_copy(hv_hbm, hvb, ld_sem.at[8]),
        pltpu.make_async_copy(w_hbm, wbuf, ld_sem.at[9]),
    ]
    for c in loads:
        c.start()

    loads[0].wait()
    pl.semaphore_wait(pltpu.get_barrier_semaphore(), nreq + nkv - 2)

    def q_copy(t):
        return pltpu.make_async_remote_copy(
            src_ref=q_all.at[0],
            dst_ref=q_all.at[slot(t)],
            send_sem=q_send.at[t],
            recv_sem=q_recv.at[t],
            device_id={"req": peer(t, -1)},
            device_id_type=MESH,
        )

    def send_q(t, carry):
        q_copy(t).start()
        return carry

    lax.fori_loop(0, nreq - 1, send_q, 0)

    def head_major(k):
        block = q_all[k]
        return [block[:, h * HD : (h + 1) * HD] for h in range(heads)]

    loads[1].wait()
    lane = lax.broadcasted_iota(jnp.int32, (nreq, nreq * rows), 1)
    row = lax.broadcasted_iota(jnp.int32, (nreq, nreq * rows), 0)
    mine = jnp.broadcast_to(task_ref[...], lane.shape) == me // HOLDERS
    mine = jnp.where(mine & (lane // rows == row), 1.0, 0.0).astype(BF16)
    er = lax.broadcasted_iota(jnp.int32, (nreq * rows, cols), 0)
    ec = lax.broadcasted_iota(jnp.int32, (nreq * rows, cols), 1)
    spread = jnp.where(er % rows == ec % rows, 1.0, 0.0).astype(BF16)
    valid[...] = jnp.dot(mine, spread, preferred_element_type=F32)

    loads[3].wait()
    loads[4].wait()
    for c in range(nch):
        at = slice(c * chunk, (c + 1) * chunk)
        vt[:HD, at] = vbuf[at, :].T
    vt[HD:, :] = jnp.ones((vt.shape[0] - HD, keys), BF16)
    loads[5].wait()
    loads[6].wait()

    def arrive(b):
        for a in range(2):
            t = 2 * b + a
            if isinstance(t, int) and t == nreq - 1:
                continue
            q_copy(t).wait_recv()

    def q_pair(b):
        return jnp.concatenate(head_major(slot(2 * b)) + head_major(slot(2 * b + 1)), 0)

    def score(c, q, sref, peaks):
        at = slice(c * chunk, (c + 1) * chunk)
        s = lax.dot_general(kbuf[at, :], q, NT, preferred_element_type=F32)
        sref[at, :] = s
        part = jnp.max(s.reshape(chunk // 8, 8, 2 * cols), axis=0)
        g = 0 if c < ncorp else 1
        peaks[g] = part if peaks[g] is None else jnp.maximum(peaks[g], part)

    def weigh(c, sref, pref, shifts):
        at = slice(c * chunk, (c + 1) * chunk)
        p = jnp.exp2(sref[at, :] * CS - shifts[0 if c < ncorp else 1])
        pref[at, :] = p.astype(BF16)

    def add_up(g, pref, acc):
        at = slice(g * deep, (g + 1) * deep)
        part = jnp.dot(vt[:, at], pref[at, :], preferred_element_type=F32)
        return part if acc is None else acc + part

    def o_copy(t):
        return pltpu.make_async_remote_copy(
            src_ref=osend.at[t],
            dst_ref=orecv.at[t],
            send_sem=o_send.at[t],
            recv_sem=o_recv.at[t],
            device_id={"req": peer(t, 1)},
            device_id_type=MESH,
        )

    def pack(lse):
        hi = lse.astype(BF16).astype(F32)
        mid = (lse - hi).astype(BF16).astype(F32)
        lo = lse - hi - mid
        sub = lax.broadcasted_iota(jnp.int32, (16, lse.shape[1]), 0)
        info = jnp.where(sub == 0, hi, jnp.where(sub == 1, mid, jnp.where(sub == 2, lo, 0.0)))
        return info.astype(BF16)

    def unpack(ref, k):
        lse = jnp.sum(ref[k, HD:, :].astype(F32), axis=0, keepdims=True)
        return ref[k, :HD, :].astype(F32), lse

    def merge(parts):
        top = functools.reduce(jnp.maximum, [v for _, v in parts])
        ws = [jnp.exp2(v - top) for _, v in parts]
        den = functools.reduce(jnp.add, ws)
        inv = 1.0 / den
        o = functools.reduce(jnp.add, [o * (w * inv) for (o, _), w in zip(parts, ws)])
        return o, top + jnp.log2(den)

    def stage(b, s_now, s_next, pref, peaks):
        mask = jnp.concatenate([valid[pl.ds(peer(2 * b + a, 1), 1), :] for a in range(2)], 1) > 0
        pk = [jnp.max(m, axis=0, keepdims=True) for m in peaks]
        top = jnp.maximum(pk[0], jnp.where(mask, pk[1], -FAR)) * CS
        shifts = [top, jnp.where(mask, top, FAR)]
        later = [None, None]
        if s_next is not None:
            arrive(b + 1)
            q = q_pair(b + 1)
        acc, done = None, 0
        for c in range(nch):
            if s_next is not None:
                score(c, q, s_next, later)
            weigh(c, s_now, pref, shifts)
            if (done + 1) * per <= c:
                acc = add_up(done, pref, acc)
                done += 1
        while done * deep < keys:
            acc = add_up(done, pref, acc)
            done += 1
        total = acc[HD : HD + 1, :]
        o = (acc[:HD, :] * (1.0 / total)).astype(BF16)
        info = pack(top + jnp.log2(total))
        for a in range(2):
            t = 2 * b + a
            at = slice(a * cols, (a + 1) * cols)
            osend[t, :HD, :] = o[:, at]
            osend[t, HD:, :] = info[:, at]
            if not isinstance(t, int) or t < nreq - 1:
                o_copy(t).start()
        return later

    arrive(0)
    peaks = [None, None]
    q0 = q_pair(0)
    for c in range(nch):
        score(c, q0, sa, peaks)

    def twice(i, peaks):
        peaks = stage(2 * i, sa, sb, pa, list(peaks))
        peaks = stage(2 * i + 1, sb, sa, pb, peaks)
        return tuple(peaks)

    nb = nreq // 2
    peaks = list(lax.fori_loop(0, nb // 2 - 1, twice, tuple(peaks)))
    peaks = stage(nb - 2, sa, sb, pa, peaks)
    stage(nb - 1, sb, None, pb, peaks)

    pr = lax.broadcasted_iota(jnp.int32, (cols, cols), 0)
    pc = lax.broadcasted_iota(jnp.int32, (cols, cols), 1)
    perm = jnp.where((pr % heads == pc // rows) & (pr // heads == pc % rows), 1.0, 0.0)
    perm16 = perm.astype(BF16)
    hq[...] = jnp.dot(perm16, jnp.concatenate(head_major(0), 0), preferred_element_type=F32)
    loads[2].wait()
    loads[7].wait()
    hcol = lax.broadcasted_iota(jnp.int32, (heads, hist), 1)
    for r in range(rows):
        at = slice(r * heads, (r + 1) * heads)
        s = lax.dot_general(
            hq[at, :].astype(BF16),
            hkb[r * hist : (r + 1) * hist, :],
            NT,
            preferred_element_type=F32,
        )
        hs[at, :] = jnp.where(hcol < len_ref[r], s, -FAR)
    s = hs[...]
    hm = jnp.max(s, axis=1, keepdims=True)
    p = jnp.exp2((s - hm) * CS)
    htot = jnp.sum(p, axis=1, keepdims=True)
    hs[...] = p
    loads[8].wait()
    for r in range(rows):
        at = slice(r * heads, (r + 1) * heads)
        hq[at, :] = jnp.dot(
            hs[at, :].astype(BF16), hvb[r * hist : (r + 1) * hist, :], preferred_element_type=F32
        )
    ho = (hq[...] * (1.0 / htot)).astype(BF16)
    hot = lax.dot_general(ho, perm16, TN, preferred_element_type=F32)
    hl = jnp.sum(perm * (hm * CS + jnp.log2(htot)), axis=0, keepdims=True)

    early = nreq - 4

    def arrived(t, carry):
        o_copy(t).wait_recv()
        return carry

    lax.fori_loop(0, early, arrived, 0)
    home = merge(
        [unpack(osend, nreq - 1), (hot, hl)] + [unpack(orecv, t) for t in range(early)]
    )
    lax.fori_loop(early, nreq - 1, arrived, 0)
    att, _ = merge([home] + [unpack(orecv, t) for t in range(early, nreq - 1)])
    att = att.T.astype(BF16)
    att = jnp.concatenate([att[h * rows : (h + 1) * rows, :] for h in range(heads)], 1)

    loads[9].wait()

    def kv_peer(e):
        dz, dc = e // 2, e % 2
        dz = dz + dz // 2 - 2 * (dz // 3)
        return ((mz + dz) % 4) * 2 + (mc + dc) % 2

    def p_copy(e):
        return pltpu.make_async_remote_copy(
            src_ref=psend.at[e],
            dst_ref=precv.at[e],
            send_sem=p_send.at[e],
            recv_sem=p_recv.at[e],
            device_id={"kvh": kv_peer(e)},
            device_id_type=MESH,
        )

    def project(e):
        at = pl.ds(pl.multiple_of(kv_peer(e) * out_w, out_w), out_w)
        return jnp.dot(att, wbuf[:, at], preferred_element_type=F32)

    def send_p(i, carry):
        e = nkv - 1 - i
        psend[e] = project(e).astype(BF16)
        p_copy(e).start()
        return carry

    lax.fori_loop(0, nkv - 1, send_p, 0)
    mixed = project(0)
    for e in (7, 6, 1, 5, 4, 3, 2):
        p_copy(e).wait_recv()
        mixed = mixed + precv[e].astype(F32)
    out_ref[...] = mixed.astype(BF16)

    def sent(t, carry):
        q_copy(t).wait_send()
        o_copy(t).wait_send()
        return carry

    lax.fori_loop(0, nreq - 1, sent, 0)

    def p_sent(e, carry):
        p_copy(e).wait_send()
        return carry

    lax.fori_loop(1, nkv, p_sent, 0)


def solution(mesh):
    nreq, nkv = mesh.shape["req"], mesh.shape["kvh"]

    def shards(q, ck, cv, tk, tv, hk, hv, lengths, task_of, w):
        rows, width = q.shape
        cols = rows * (width // HD)
        keys = ck.shape[0] + tk.shape[0]
        hist = hk.shape[0] // rows
        out_w = w.shape[1] // nkv
        hbm = pl.BlockSpec(memory_space=pl.ANY)
        vmem = pl.BlockSpec(memory_space=pltpu.VMEM)
        dma = pltpu.SemaphoreType.DMA
        return pl.pallas_call(
            kernel,
            out_shape=jax.ShapeDtypeStruct((rows, out_w), BF16),
            in_specs=[hbm] * 10,
            out_specs=vmem,
            scratch_shapes=[
                pltpu.VMEM((nreq, rows, width), BF16),
                pltpu.VMEM((keys, HD), BF16),
                pltpu.VMEM((keys, HD), BF16),
                pltpu.VMEM((HD + 16, keys), BF16),
                pltpu.VMEM(hk.shape, BF16),
                pltpu.VMEM(hv.shape, BF16),
                pltpu.SMEM(lengths.shape, jnp.int32),
                pltpu.VMEM((1, nreq * rows), jnp.int32),
                pltpu.VMEM(w.shape, BF16),
                pltpu.VMEM((keys, 2 * cols), F32),
                pltpu.VMEM((keys, 2 * cols), F32),
                pltpu.VMEM((keys, 2 * cols), BF16),
                pltpu.VMEM((keys, 2 * cols), BF16),
                pltpu.VMEM((nreq, HD + 16, cols), BF16),
                pltpu.VMEM((nreq, HD + 16, cols), BF16),
                pltpu.VMEM((cols, hist), F32),
                pltpu.VMEM((cols, HD), F32),
                pltpu.VMEM((nreq, cols), F32),
                pltpu.VMEM((nkv, rows, out_w), BF16),
                pltpu.VMEM((nkv, rows, out_w), BF16),
                dma((10,)),
                dma((nreq,)),
                dma((nreq,)),
                dma((nreq,)),
                dma((nreq,)),
                dma((nkv,)),
                dma((nkv,)),
            ],
            compiler_params=pltpu.CompilerParams(
                collective_id=0, has_side_effects=True, vmem_limit_bytes=60 * 2**20
            ),
        )(q, ck, cv, tk, tv, hk, hv, lengths, task_of.reshape(1, -1), w)

    return jax.shard_map(
        shards,
        mesh=mesh,
        in_specs=(P("req", "kvh"),) * 7 + (P("req"), P(), P("kvh", None)),
        out_specs=P("req", "kvh"),
        check_vma=False,
    )
```

```python
import functools
import math

import jax
import jax.numpy as jnp
from jax import lax
from jax.experimental import pallas as pl
from jax.experimental.pallas import tpu as pltpu
from jax.sharding import PartitionSpec as P

HD = 128
HOLDERS = 2
MESH = pl.DeviceIdType.MESH
F32 = jnp.float32
BF16 = jnp.bfloat16
CS = math.log2(math.e) / math.sqrt(HD)
FAR = 1e30
NT = (((1,), (1,)), ((), ()))
TN = (((0,), (0,)), ((), ()))


def kernel(
    q_hbm,
    ck_hbm,
    cv_hbm,
    tk_hbm,
    tv_hbm,
    hk_hbm,
    hv_hbm,
    len_hbm,
    task_hbm,
    w_hbm,
    out_ref,
    q_all,
    kbuf,
    vbuf,
    vt,
    hkb,
    hvb,
    len_ref,
    task_ref,
    wbuf,
    sa,
    sb,
    pa,
    pb,
    osend,
    orecv,
    hs,
    hq,
    valid,
    psend,
    ld_sem,
    q_send,
    q_recv,
    o_send,
    o_recv,
    p_send,
    p_recv,
):
    nreq, rows, width = q_all.shape
    nkv = psend.shape[0]
    heads = width // HD
    cols = rows * heads
    corpus = ck_hbm.shape[0]
    keys = kbuf.shape[0]
    hist = hkb.shape[0] // rows
    out_w = psend.shape[2]
    chunk, deep = 512, 2048
    nch, ncorp, per = keys // chunk, corpus // chunk, deep // chunk
    me = lax.axis_index("req")
    mj = lax.axis_index("kvh")
    y, x = me // 4, me % 4
    mz, mc = mj // 2, mj % 2

    def off(t):
        dy = 3 - t // 4
        return dy, (t % 4 + 1 + dy) % 4

    def slot(t):
        dy, dx = off(t)
        return dy * 4 + dx

    def peer(t, sign):
        dy, dx = off(t)
        return ((y + 4 + sign * dy) % 4) * 4 + (x + 4 + sign * dx) % 4

    def greet(**device):
        pl.semaphore_signal(
            pltpu.get_barrier_semaphore(), inc=1, device_id=device, device_id_type=MESH
        )

    def greet_req(t, carry):
        greet(req=peer(t, -1))
        return carry

    lax.fori_loop(0, nreq - 1, greet_req, 0)

    def greet_kv(e, carry):
        greet(kvh=(mj + e) % nkv)
        return carry

    lax.fori_loop(1, nkv, greet_kv, 0)

    loads = [
        pltpu.make_async_copy(q_hbm, q_all.at[0], ld_sem.at[0]),
        pltpu.make_async_copy(task_hbm, task_ref, ld_sem.at[1]),
        pltpu.make_async_copy(len_hbm, len_ref, ld_sem.at[2]),
        pltpu.make_async_copy(cv_hbm, vbuf.at[pl.ds(0, corpus)], ld_sem.at[3]),
        pltpu.make_async_copy(tv_hbm, vbuf.at[pl.ds(corpus, keys - corpus)], ld_sem.at[4]),
        pltpu.make_async_copy(ck_hbm, kbuf.at[pl.ds(0, corpus)], ld_sem.at[5]),
        pltpu.make_async_copy(tk_hbm, kbuf.at[pl.ds(corpus, keys - corpus)], ld_sem.at[6]),
        pltpu.make_async_copy(hk_hbm, hkb, ld_sem.at[7]),
        pltpu.make_async_copy(hv_hbm, hvb, ld_sem.at[8]),
        pltpu.make_async_copy(w_hbm, wbuf, ld_sem.at[9]),
    ]
    for c in loads:
        c.start()

    loads[0].wait()
    pl.semaphore_wait(pltpu.get_barrier_semaphore(), nreq + nkv - 2)

    def q_copy(t):
        return pltpu.make_async_remote_copy(
            src_ref=q_all.at[0],
            dst_ref=q_all.at[slot(t)],
            send_sem=q_send,
            recv_sem=q_recv.at[t],
            device_id={"req": peer(t, -1)},
            device_id_type=MESH,
        )

    def send_q(t, carry):
        q_copy(t).start()
        return carry

    lax.fori_loop(0, nreq - 1, send_q, 0)

    def head_major(k):
        block = q_all[k]
        return [block[:, h * HD : (h + 1) * HD] for h in range(heads)]

    loads[1].wait()
    lane = lax.broadcasted_iota(jnp.int32, (nreq, nreq * rows), 1)
    row = lax.broadcasted_iota(jnp.int32, (nreq, nreq * rows), 0)
    mine = jnp.broadcast_to(task_ref[...], lane.shape) == me // HOLDERS
    mine = jnp.where(mine & (lane // rows == row), 1.0, 0.0).astype(BF16)
    er = lax.broadcasted_iota(jnp.int32, (nreq * rows, cols), 0)
    ec = lax.broadcasted_iota(jnp.int32, (nreq * rows, cols), 1)
    spread = jnp.where(er % rows == ec % rows, 1.0, 0.0).astype(BF16)
    valid[...] = jnp.dot(mine, spread, preferred_element_type=F32)

    loads[3].wait()
    loads[4].wait()
    for c in range(nch):
        at = slice(c * chunk, (c + 1) * chunk)
        vt[:HD, at] = vbuf[at, :].T
    vt[HD:, :] = jnp.ones((vt.shape[0] - HD, keys), BF16)
    loads[5].wait()
    loads[6].wait()

    early = nreq - 4

    def arrive(block):
        for t in block:
            q_copy(t).wait_recv()

    def q_of(block):
        return jnp.concatenate([tile for t in block for tile in head_major(slot(t))], 0)

    def score(c, q, sref, peaks):
        at = slice(c * chunk, (c + 1) * chunk)
        s = lax.dot_general(kbuf[at, :], q, NT, preferred_element_type=F32)
        sref[at, : s.shape[1]] = s
        part = jnp.max(s.reshape(chunk // 8, 8, s.shape[1]), axis=0)
        g = 0 if c < ncorp else 1
        peaks[g] = part if peaks[g] is None else jnp.maximum(peaks[g], part)

    def weigh(c, sref, pref, shifts):
        at = slice(c * chunk, (c + 1) * chunk)
        n = shifts[0].shape[1]
        p = jnp.exp2(sref[at, :n] * CS - shifts[0 if c < ncorp else 1])
        pref[at, :n] = p.astype(BF16)

    def add_up(g, pref, n, acc):
        at = slice(g * deep, (g + 1) * deep)
        part = jnp.dot(vt[:, at], pref[at, :n], preferred_element_type=F32)
        return part if acc is None else acc + part

    def o_copy(t):
        return pltpu.make_async_remote_copy(
            src_ref=osend.at[t],
            dst_ref=orecv.at[t],
            send_sem=o_send,
            recv_sem=o_recv.at[t // early],
            device_id={"req": peer(t, 1)},
            device_id_type=MESH,
        )

    def pack(lse):
        hi = lse.astype(BF16).astype(F32)
        mid = (lse - hi).astype(BF16).astype(F32)
        lo = lse - hi - mid
        sub = lax.broadcasted_iota(jnp.int32, (16, lse.shape[1]), 0)
        info = jnp.where(sub == 0, hi, jnp.where(sub == 1, mid, jnp.where(sub == 2, lo, 0.0)))
        return info.astype(BF16)

    def unpack(ref, k):
        lse = jnp.sum(ref[k, HD:, :].astype(F32), axis=0, keepdims=True)
        return ref[k, :HD, :].astype(F32), lse

    def merge(parts):
        top = functools.reduce(jnp.maximum, [v for _, v in parts])
        ws = [jnp.exp2(v - top) for _, v in parts]
        den = functools.reduce(jnp.add, ws)
        inv = 1.0 / den
        o = functools.reduce(jnp.add, [o * (w * inv) for (o, _), w in zip(parts, ws)])
        return o, top + jnp.log2(den)

    def stage(now, then, s_now, s_then, pref, peaks):
        n = len(now) * cols
        mask = jnp.concatenate([valid[pl.ds(peer(t, 1), 1), :] for t in now], 1) > 0
        pk = [jnp.max(m, axis=0, keepdims=True) for m in peaks]
        top = jnp.maximum(pk[0], jnp.where(mask, pk[1], -FAR)) * CS
        shifts = [top, jnp.where(mask, top, FAR)]
        later = [None, None]
        if then:
            arrive(then)
            q = q_of(then)
        acc, done = None, 0
        for c in range(nch):
            if then:
                score(c, q, s_then, later)
            weigh(c, s_now, pref, shifts)
            if (done + 1) * per <= c:
                acc = add_up(done, pref, n, acc)
                done += 1
        while done * deep < keys:
            acc = add_up(done, pref, n, acc)
            done += 1
        total = acc[HD : HD + 1, :]
        o = (acc[:HD, :] * (1.0 / total)).astype(BF16)
        info = pack(top + jnp.log2(total))
        for a, t in enumerate(now):
            at = slice(a * cols, (a + 1) * cols)
            osend[t, :HD, :] = o[:, at]
            osend[t, HD:, :] = info[:, at]
            if not isinstance(t, int) or t < nreq - 1:
                o_copy(t).start()
        return later

    def first_scores(block, sref):
        peaks = [None, None]
        q = q_of(block)
        for c in range(nch):
            score(c, q, sref, peaks)
        return peaks

    stage([nreq - 1], None, sb, None, pb, first_scores([nreq - 1], sb))

    pr = lax.broadcasted_iota(jnp.int32, (cols, cols), 0)
    pc = lax.broadcasted_iota(jnp.int32, (cols, cols), 1)
    perm = jnp.where((pr % heads == pc // rows) & (pr // heads == pc % rows), 1.0, 0.0)
    perm16 = perm.astype(BF16)
    hq[...] = jnp.dot(perm16, jnp.concatenate(head_major(0), 0), preferred_element_type=F32)
    loads[2].wait()
    loads[7].wait()
    hcol = lax.broadcasted_iota(jnp.int32, (heads, hist), 1)
    for r in range(rows):
        at = slice(r * heads, (r + 1) * heads)
        s = lax.dot_general(
            hq[at, :].astype(BF16),
            hkb[r * hist : (r + 1) * hist, :],
            NT,
            preferred_element_type=F32,
        )
        hs[at, :] = jnp.where(hcol < len_ref[r], s, -FAR)
    s = hs[...]
    hm = jnp.max(s, axis=1, keepdims=True)
    p = jnp.exp2((s - hm) * CS)
    htot = jnp.sum(p, axis=1, keepdims=True)
    hs[...] = p
    loads[8].wait()
    for r in range(rows):
        at = slice(r * heads, (r + 1) * heads)
        hq[at, :] = jnp.dot(
            hs[at, :].astype(BF16), hvb[r * hist : (r + 1) * hist, :], preferred_element_type=F32
        )
    ho = (hq[...] * (1.0 / htot)).astype(BF16)
    hot = lax.dot_general(ho, perm16, TN, preferred_element_type=F32)
    hl = jnp.sum(perm * (hm * CS + jnp.log2(htot)), axis=0, keepdims=True)

    arrive([0, 1])
    peaks = first_scores([0, 1], sa)

    def twice(i, peaks):
        t = 4 * i
        peaks = stage([t, t + 1], [t + 2, t + 3], sa, sb, pa, list(peaks))
        peaks = stage([t + 2, t + 3], [t + 4, t + 5], sb, sa, pb, peaks)
        return tuple(peaks)

    peaks = list(lax.fori_loop(0, nreq // 4 - 1, twice, tuple(peaks)))
    peaks = stage([nreq - 4, nreq - 3], [nreq - 2], sa, sb, pa, peaks)
    stage([nreq - 2], None, sb, None, pb, peaks)

    def arrived(t, n):
        pltpu.make_async_remote_copy(
            src_ref=osend.at[pl.ds(t, n)],
            dst_ref=orecv.at[pl.ds(t, n)],
            send_sem=o_send,
            recv_sem=o_recv.at[t // early],
            device_id={"req": peer(0, 1)},
            device_id_type=MESH,
        ).wait_recv()

    arrived(0, early)
    home = merge(
        [unpack(osend, nreq - 1), (hot, hl)] + [unpack(orecv, t) for t in range(early)]
    )
    arrived(early, 3)
    att, _ = merge([home] + [unpack(orecv, t) for t in range(early, nreq - 1)])
    att = att.T.astype(BF16)
    att = jnp.concatenate([att[h * rows : (h + 1) * rows, :] for h in range(heads)], 1)

    loads[9].wait()

    def kv_peer(e):
        dz, dc = e // 2, e % 2
        dz = dz + dz // 2 - 2 * (dz // 3)
        return ((mz + dz) % 4) * 2 + (mc + dc) % 2

    def p_copy(e):
        return pltpu.make_async_remote_copy(
            src_ref=psend.at[e],
            dst_ref=out_ref.at[e],
            send_sem=p_send,
            recv_sem=p_recv,
            device_id={"kvh": kv_peer(e)},
            device_id_type=MESH,
        )

    def project(e):
        at = pl.ds(pl.multiple_of(kv_peer(e) * out_w, out_w), out_w)
        return jnp.dot(att, wbuf[:, at], preferred_element_type=F32)

    def send_p(i, carry):
        e = nkv - 1 - i
        psend[e] = project(e).astype(BF16)
        p_copy(e).start()
        return carry

    lax.fori_loop(0, nkv - 1, send_p, 0)
    psend[0] = project(0).astype(BF16)
    keep = pltpu.make_async_copy(psend.at[0], out_ref.at[0], ld_sem.at[1])
    keep.start()

    def whole(src, dst, send_sem, recv_sem):
        return pltpu.make_async_remote_copy(
            src_ref=src,
            dst_ref=dst,
            send_sem=send_sem,
            recv_sem=recv_sem,
            device_id={"kvh": kv_peer(1)},
            device_id_type=MESH,
        )

    others = pl.ds(1, nreq - 1)
    whole(q_all.at[others], q_all.at[others], q_send, q_recv.at[0]).wait_send()
    whole(osend.at[others], orecv.at[others], o_send, o_recv.at[0]).wait_send()
    parts = whole(psend.at[pl.ds(1, nkv - 1)], out_ref.at[pl.ds(1, nkv - 1)], p_send, p_recv)
    parts.wait_send()
    parts.wait_recv()
    keep.wait()


def solution(mesh):
    nreq, nkv = mesh.shape["req"], mesh.shape["kvh"]

    def shards(q, ck, cv, tk, tv, hk, hv, lengths, task_of, w):
        rows, width = q.shape
        cols = rows * (width // HD)
        keys = ck.shape[0] + tk.shape[0]
        hist = hk.shape[0] // rows
        out_w = w.shape[1] // nkv
        hbm = pl.BlockSpec(memory_space=pl.ANY)
        dma = pltpu.SemaphoreType.DMA
        parts = pl.pallas_call(
            kernel,
            out_shape=jax.ShapeDtypeStruct((nkv, rows, out_w), BF16),
            in_specs=[hbm] * 10,
            out_specs=hbm,
            scratch_shapes=[
                pltpu.VMEM((nreq, rows, width), BF16),
                pltpu.VMEM((keys, HD), BF16),
                pltpu.VMEM((keys, HD), BF16),
                pltpu.VMEM((HD + 16, keys), BF16),
                pltpu.VMEM(hk.shape, BF16),
                pltpu.VMEM(hv.shape, BF16),
                pltpu.SMEM(lengths.shape, jnp.int32),
                pltpu.VMEM((1, nreq * rows), jnp.int32),
                pltpu.VMEM(w.shape, BF16),
                pltpu.VMEM((keys, 2 * cols), F32),
                pltpu.VMEM((keys, 2 * cols), F32),
                pltpu.VMEM((keys, 2 * cols), BF16),
                pltpu.VMEM((keys, 2 * cols), BF16),
                pltpu.VMEM((nreq, HD + 16, cols), BF16),
                pltpu.VMEM((nreq, HD + 16, cols), BF16),
                pltpu.VMEM((cols, hist), F32),
                pltpu.VMEM((cols, HD), F32),
                pltpu.VMEM((nreq, cols), F32),
                pltpu.VMEM((nkv, rows, out_w), BF16),
                dma((10,)),
                dma,
                dma((nreq - 1,)),
                dma,
                dma((2,)),
                dma,
                dma,
            ],
            compiler_params=pltpu.CompilerParams(
                collective_id=0, has_side_effects=True, vmem_limit_bytes=60 * 2**20
            ),
        )(q, ck, cv, tk, tv, hk, hv, lengths, task_of.reshape(1, -1), w)
        return jnp.sum(parts.astype(F32), axis=0).astype(BF16)

    return jax.shard_map(
        shards,
        mesh=mesh,
        in_specs=(P("req", "kvh"),) * 7 + (P("req"), P(), P("kvh", None)),
        out_specs=P("req", "kvh"),
        check_vma=False,
    )
```

```python
import functools
import math

import jax
import jax.numpy as jnp
from jax import lax
from jax.experimental import pallas as pl
from jax.experimental.pallas import tpu as pltpu
from jax.sharding import PartitionSpec as P

HD = 128
HOLDERS = 2
MESH = pl.DeviceIdType.MESH
F32 = jnp.float32
BF16 = jnp.bfloat16
CS = math.log2(math.e) / math.sqrt(HD)
FAR = 1e30
NT = (((1,), (1,)), ((), ()))
TN = (((0,), (0,)), ((), ()))


def kernel(
    q_hbm,
    ck_hbm,
    cv_hbm,
    tk_hbm,
    tv_hbm,
    hk_hbm,
    hv_hbm,
    len_hbm,
    task_hbm,
    w_hbm,
    out_ref,
    q_all,
    kbuf,
    vbuf,
    vt,
    hkb,
    hvb,
    len_ref,
    task_ref,
    wbuf,
    sa,
    sb,
    pa,
    pb,
    osend,
    orecv,
    hs,
    hq,
    valid,
    psend,
    ld_sem,
    q_send,
    q_recv,
    o_send,
    o_recv,
    p_send,
    p_recv,
):
    nreq, rows, width = q_all.shape
    nkv = psend.shape[0]
    heads = width // HD
    cols = rows * heads
    corpus = ck_hbm.shape[0]
    keys = kbuf.shape[0]
    hist = hkb.shape[0] // rows
    out_w = psend.shape[2]
    chunk, deep = 512, 2048
    nch, ncorp, per = keys // chunk, corpus // chunk, deep // chunk
    me = lax.axis_index("req")
    mj = lax.axis_index("kvh")
    y, x = lax.div(me, 4), lax.rem(me, 4)
    mz, mc = lax.div(mj, 2), lax.rem(mj, 2)

    def rem4(v):
        return v % 4 if isinstance(v, int) else lax.rem(v, 4)

    def number(block):
        return 4 * block[0] + block[1]

    def slot(block):
        g, a = block
        return (3 - g) * 4 + rem4(a + 4 - g)

    def source(block):
        g, a = block
        return rem4(y + 3 - g) * 4 + rem4(x + a + 4 - g)

    def reader(block):
        g, a = block
        return rem4(y + 1 + g) * 4 + rem4(x + 4 - a + g)

    others = [(g, a) for g in range(4) for a in range(4)][:-1]

    def greet(**device):
        pl.semaphore_signal(
            pltpu.get_barrier_semaphore(), inc=1, device_id=device, device_id_type=MESH
        )

    for block in others:
        greet(req=reader(block))
    for e in range(1, nkv):
        greet(kvh=lax.rem(mj + e, nkv))

    loads = [
        pltpu.make_async_copy(q_hbm, q_all.at[0], ld_sem.at[0]),
        pltpu.make_async_copy(task_hbm, task_ref, ld_sem.at[1]),
        pltpu.make_async_copy(len_hbm, len_ref, ld_sem.at[2]),
        pltpu.make_async_copy(cv_hbm, vbuf.at[pl.ds(0, corpus)], ld_sem.at[3]),
        pltpu.make_async_copy(tv_hbm, vbuf.at[pl.ds(corpus, keys - corpus)], ld_sem.at[4]),
        pltpu.make_async_copy(ck_hbm, kbuf.at[pl.ds(0, corpus)], ld_sem.at[5]),
        pltpu.make_async_copy(tk_hbm, kbuf.at[pl.ds(corpus, keys - corpus)], ld_sem.at[6]),
        pltpu.make_async_copy(hk_hbm, hkb, ld_sem.at[7]),
        pltpu.make_async_copy(hv_hbm, hvb, ld_sem.at[8]),
        pltpu.make_async_copy(w_hbm, wbuf, ld_sem.at[9]),
    ]
    for c in loads:
        c.start()

    loads[0].wait()
    pl.semaphore_wait(pltpu.get_barrier_semaphore(), nreq + nkv - 2)

    def q_copy(block):
        return pltpu.make_async_remote_copy(
            src_ref=q_all.at[0],
            dst_ref=q_all.at[slot(block)],
            send_sem=q_send,
            recv_sem=q_recv.at[number(block)],
            device_id={"req": reader(block)},
            device_id_type=MESH,
        )

    for block in others:
        q_copy(block).start()

    def head_major(k):
        block = q_all[k]
        return [block[:, h * HD : (h + 1) * HD] for h in range(heads)]

    loads[1].wait()
    lane = lax.broadcasted_iota(jnp.int32, (nreq, nreq * rows), 1)
    row = lax.broadcasted_iota(jnp.int32, (nreq, nreq * rows), 0)
    mine = jnp.broadcast_to(task_ref[...], lane.shape) == me // HOLDERS
    mine = jnp.where(mine & (lane // rows == row), 1.0, 0.0).astype(BF16)
    er = lax.broadcasted_iota(jnp.int32, (nreq * rows, cols), 0)
    ec = lax.broadcasted_iota(jnp.int32, (nreq * rows, cols), 1)
    spread = jnp.where(er % rows == ec % rows, 1.0, 0.0).astype(BF16)
    valid[...] = jnp.dot(mine, spread, preferred_element_type=F32)

    loads[3].wait()
    loads[4].wait()
    for c in range(nch):
        at = slice(c * chunk, (c + 1) * chunk)
        vt[:HD, at] = vbuf[at, :].T
    vt[HD:, :] = jnp.ones((vt.shape[0] - HD, keys), BF16)
    loads[5].wait()
    loads[6].wait()

    early = nreq - 4

    def arrive(blocks):
        for block in blocks:
            q_copy(block).wait_recv()

    def q_of(blocks):
        return jnp.concatenate([tile for b in blocks for tile in head_major(slot(b))], 0)

    def score(c, q, sref, peaks):
        at = slice(c * chunk, (c + 1) * chunk)
        s = lax.dot_general(kbuf[at, :], q, NT, preferred_element_type=F32)
        sref[at, : s.shape[1]] = s
        part = jnp.max(s.reshape(chunk // 8, 8, s.shape[1]), axis=0)
        g = 0 if c < ncorp else 1
        peaks[g] = part if peaks[g] is None else jnp.maximum(peaks[g], part)

    def weigh(c, sref, pref, shifts):
        at = slice(c * chunk, (c + 1) * chunk)
        n = shifts[0].shape[1]
        p = jnp.exp2(sref[at, :n] * CS - shifts[0 if c < ncorp else 1])
        pref[at, :n] = p.astype(BF16)

    def add_up(g, pref, n, acc):
        at = slice(g * deep, (g + 1) * deep)
        part = jnp.dot(vt[:, at], pref[at, :n], preferred_element_type=F32)
        return part if acc is None else acc + part

    def o_copy(block):
        t = number(block)
        return pltpu.make_async_remote_copy(
            src_ref=osend.at[t],
            dst_ref=orecv.at[t],
            send_sem=o_send,
            recv_sem=o_recv.at[1 if isinstance(t, int) and t >= early else 0],
            device_id={"req": source(block)},
            device_id_type=MESH,
        )

    def pack(lse):
        hi = lse.astype(BF16).astype(F32)
        mid = (lse - hi).astype(BF16).astype(F32)
        lo = lse - hi - mid
        sub = lax.broadcasted_iota(jnp.int32, (16, lse.shape[1]), 0)
        info = jnp.where(sub == 0, hi, jnp.where(sub == 1, mid, jnp.where(sub == 2, lo, 0.0)))
        return info.astype(BF16)

    def unpack(ref, k):
        lse = jnp.sum(ref[k, HD:, :].astype(F32), axis=0, keepdims=True)
        return ref[k, :HD, :].astype(F32), lse

    def merge(parts):
        top = functools.reduce(jnp.maximum, [v for _, v in parts])
        ws = [jnp.exp2(v - top) for _, v in parts]
        den = functools.reduce(jnp.add, ws)
        inv = 1.0 / den
        o = functools.reduce(jnp.add, [o * (w * inv) for (o, _), w in zip(parts, ws)])
        return o, top + jnp.log2(den)

    def stage(now, then, s_now, s_then, pref, peaks):
        n = len(now) * cols
        mask = jnp.concatenate([valid[pl.ds(source(b), 1), :] for b in now], 1) > 0
        pk = [jnp.max(m, axis=0, keepdims=True) for m in peaks]
        top = jnp.maximum(pk[0], jnp.where(mask, pk[1], -FAR)) * CS
        shifts = [top, jnp.where(mask, top, FAR)]
        later = [None, None]
        if then:
            arrive(then)
            q = q_of(then)
        acc, done = None, 0
        for c in range(nch):
            if then:
                score(c, q, s_then, later)
            weigh(c, s_now, pref, shifts)
            if (done + 1) * per <= c:
                acc = add_up(done, pref, n, acc)
                done += 1
        while done * deep < keys:
            acc = add_up(done, pref, n, acc)
            done += 1
        total = acc[HD : HD + 1, :]
        o = (acc[:HD, :] * (1.0 / total)).astype(BF16)
        info = pack(top + jnp.log2(total))
        for i, block in enumerate(now):
            at = slice(i * cols, (i + 1) * cols)
            t = number(block)
            osend[t, :HD, :] = o[:, at]
            osend[t, HD:, :] = info[:, at]
            if not isinstance(t, int) or t < nreq - 1:
                o_copy(block).start()
        return later

    def first_scores(blocks, sref):
        peaks = [None, None]
        q = q_of(blocks)
        for c in range(nch):
            score(c, q, sref, peaks)
        return peaks

    stage([(3, 3)], None, sb, None, pb, first_scores([(3, 3)], sb))

    pr = lax.broadcasted_iota(jnp.int32, (cols, cols), 0)
    pc = lax.broadcasted_iota(jnp.int32, (cols, cols), 1)
    perm = jnp.where((pr % heads == pc // rows) & (pr // heads == pc % rows), 1.0, 0.0)
    perm16 = perm.astype(BF16)
    hq[...] = jnp.dot(perm16, jnp.concatenate(head_major(0), 0), preferred_element_type=F32)
    loads[2].wait()
    loads[7].wait()
    hcol = lax.broadcasted_iota(jnp.int32, (heads, hist), 1)
    for r in range(rows):
        at = slice(r * heads, (r + 1) * heads)
        s = lax.dot_general(
            hq[at, :].astype(BF16),
            hkb[r * hist : (r + 1) * hist, :],
            NT,
            preferred_element_type=F32,
        )
        hs[at, :] = jnp.where(hcol < len_ref[r], s, -FAR)
    s = hs[...]
    hm = jnp.max(s, axis=1, keepdims=True)
    p = jnp.exp2((s - hm) * CS)
    htot = jnp.sum(p, axis=1, keepdims=True)
    hs[...] = p
    loads[8].wait()
    for r in range(rows):
        at = slice(r * heads, (r + 1) * heads)
        hq[at, :] = jnp.dot(
            hs[at, :].astype(BF16), hvb[r * hist : (r + 1) * hist, :], preferred_element_type=F32
        )
    ho = (hq[...] * (1.0 / htot)).astype(BF16)
    hot = lax.dot_general(ho, perm16, TN, preferred_element_type=F32)
    hl = jnp.sum(perm * (hm * CS + jnp.log2(htot)), axis=0, keepdims=True)

    arrive([(0, 0), (0, 1)])
    peaks = first_scores([(0, 0), (0, 1)], sa)

    def twice(g, peaks):
        peaks = stage([(g, 0), (g, 1)], [(g, 2), (g, 3)], sa, sb, pa, list(peaks))
        peaks = stage([(g, 2), (g, 3)], [(g + 1, 0), (g + 1, 1)], sb, sa, pb, peaks)
        return tuple(peaks)

    peaks = list(lax.fori_loop(0, 3, twice, tuple(peaks)))
    peaks = stage([(3, 0), (3, 1)], [(3, 2)], sa, sb, pa, peaks)
    stage([(3, 2)], None, sb, None, pb, peaks)

    def arrived(t, n):
        pltpu.make_async_remote_copy(
            src_ref=osend.at[pl.ds(t, n)],
            dst_ref=orecv.at[pl.ds(t, n)],
            send_sem=o_send,
            recv_sem=o_recv.at[t // early],
            device_id={"req": source((0, 0))},
            device_id_type=MESH,
        ).wait_recv()

    arrived(0, early)
    home = merge(
        [unpack(osend, nreq - 1), (hot, hl)] + [unpack(orecv, t) for t in range(early)]
    )
    arrived(early, 3)
    att, _ = merge([home] + [unpack(orecv, t) for t in range(early, nreq - 1)])
    att = att.T.astype(BF16)
    att = jnp.concatenate([att[h * rows : (h + 1) * rows, :] for h in range(heads)], 1)

    loads[9].wait()

    def kv_peer(e):
        if isinstance(e, int):
            dz, dc = (0, 1, 3, 2)[e // 2], e % 2
        else:
            half, dc = lax.div(e, 2), lax.rem(e, 2)
            dz = half + lax.div(half, 2) - 2 * lax.div(half, 3)
        return lax.rem(mz + dz, 4) * 2 + lax.rem(mc + dc, 2)

    def p_copy(e):
        return pltpu.make_async_remote_copy(
            src_ref=psend.at[e],
            dst_ref=out_ref.at[e],
            send_sem=p_send,
            recv_sem=p_recv,
            device_id={"kvh": kv_peer(e)},
            device_id_type=MESH,
        )

    def project(e):
        at = pl.ds(pl.multiple_of(kv_peer(e) * out_w, out_w), out_w)
        return jnp.dot(att, wbuf[:, at], preferred_element_type=F32)

    def send_p(i, carry):
        e = nkv - 1 - i
        psend[e] = project(e).astype(BF16)
        p_copy(e).start()
        return carry

    lax.fori_loop(0, nkv - 1, send_p, 0)
    psend[0] = project(0).astype(BF16)
    keep = pltpu.make_async_copy(psend.at[0], out_ref.at[0], ld_sem.at[1])
    keep.start()

    def whole(src, dst, send_sem, recv_sem):
        return pltpu.make_async_remote_copy(
            src_ref=src,
            dst_ref=dst,
            send_sem=send_sem,
            recv_sem=recv_sem,
            device_id={"kvh": kv_peer(1)},
            device_id_type=MESH,
        )

    most = pl.ds(0, nreq - 1)
    whole(q_all.at[most], q_all.at[most], q_send, q_recv.at[0]).wait_send()
    whole(osend.at[most], orecv.at[most], o_send, o_recv.at[0]).wait_send()
    parts = whole(psend.at[pl.ds(1, nkv - 1)], out_ref.at[pl.ds(1, nkv - 1)], p_send, p_recv)
    parts.wait_send()
    parts.wait_recv()
    keep.wait()


def solution(mesh):
    nreq, nkv = mesh.shape["req"], mesh.shape["kvh"]

    def shards(q, ck, cv, tk, tv, hk, hv, lengths, task_of, w):
        rows, width = q.shape
        cols = rows * (width // HD)
        keys = ck.shape[0] + tk.shape[0]
        hist = hk.shape[0] // rows
        out_w = w.shape[1] // nkv
        hbm = pl.BlockSpec(memory_space=pl.ANY)
        dma = pltpu.SemaphoreType.DMA
        parts = pl.pallas_call(
            kernel,
            out_shape=jax.ShapeDtypeStruct((nkv, rows, out_w), BF16),
            in_specs=[hbm] * 10,
            out_specs=hbm,
            scratch_shapes=[
                pltpu.VMEM((nreq, rows, width), BF16),
                pltpu.VMEM((keys, HD), BF16),
                pltpu.VMEM((keys, HD), BF16),
                pltpu.VMEM((HD + 16, keys), BF16),
                pltpu.VMEM(hk.shape, BF16),
                pltpu.VMEM(hv.shape, BF16),
                pltpu.SMEM(lengths.shape, jnp.int32),
                pltpu.VMEM((1, nreq * rows), jnp.int32),
                pltpu.VMEM(w.shape, BF16),
                pltpu.VMEM((keys, 2 * cols), F32),
                pltpu.VMEM((keys, 2 * cols), F32),
                pltpu.VMEM((keys, 2 * cols), BF16),
                pltpu.VMEM((keys, 2 * cols), BF16),
                pltpu.VMEM((nreq, HD + 16, cols), BF16),
                pltpu.VMEM((nreq, HD + 16, cols), BF16),
                pltpu.VMEM((cols, hist), F32),
                pltpu.VMEM((cols, HD), F32),
                pltpu.VMEM((nreq, cols), F32),
                pltpu.VMEM((nkv, rows, out_w), BF16),
                dma((10,)),
                dma,
                dma((nreq - 1,)),
                dma,
                dma((2,)),
                dma,
                dma,
            ],
            compiler_params=pltpu.CompilerParams(
                collective_id=0, has_side_effects=True, vmem_limit_bytes=60 * 2**20
            ),
        )(q, ck, cv, tk, tv, hk, hv, lengths, task_of.reshape(1, -1), w)
        return jnp.sum(parts.astype(F32), axis=0).astype(BF16)

    return jax.shard_map(
        shards,
        mesh=mesh,
        in_specs=(P("req", "kvh"),) * 7 + (P("req"), P(), P("kvh", None)),
        out_specs=P("req", "kvh"),
        check_vma=False,
    )
```

```python
import functools
import math

import jax
import jax.numpy as jnp
from jax import lax
from jax.experimental import pallas as pl
from jax.experimental.pallas import tpu as pltpu
from jax.sharding import PartitionSpec as P

HD = 128
HOLDERS = 2
MESH = pl.DeviceIdType.MESH
F32 = jnp.float32
BF16 = jnp.bfloat16
CS = math.log2(math.e) / math.sqrt(HD)
FAR = 1e30
NT = (((1,), (1,)), ((), ()))
TN = (((0,), (0,)), ((), ()))


def kernel(
    q_hbm,
    ck_hbm,
    cv_hbm,
    tk_hbm,
    tv_hbm,
    hk_hbm,
    hv_hbm,
    len_hbm,
    task_hbm,
    w_hbm,
    out_ref,
    q_all,
    kbuf,
    vbuf,
    vt,
    hkb,
    hvb,
    len_ref,
    task_ref,
    wbuf,
    sa,
    sb,
    pa,
    pb,
    osend,
    orecv,
    hs,
    hq,
    valid,
    psend,
    ld_sem,
    q_send,
    q_recv,
    o_send,
    o_recv,
    p_send,
    p_recv,
):
    nreq, rows, width = q_all.shape
    nkv = psend.shape[0]
    heads = width // HD
    cols = rows * heads
    corpus = ck_hbm.shape[0]
    keys = kbuf.shape[0]
    hist = hkb.shape[0] // rows
    out_w = psend.shape[2]
    chunk, deep = 512, 2048
    nch, ncorp, per = keys // chunk, corpus // chunk, deep // chunk
    me = lax.axis_index("req")
    mj = lax.axis_index("kvh")
    y, x = lax.div(me, 4), lax.rem(me, 4)
    mz, mc = lax.div(mj, 2), lax.rem(mj, 2)

    def rem4(v):
        return v % 4 if isinstance(v, int) else lax.rem(v, 4)

    def number(block):
        return 4 * block[0] + block[1]

    def slot(block):
        g, a = block
        return (3 - g) * 4 + rem4(a + 4 - g)

    def source(block):
        g, a = block
        return rem4(y + 3 - g) * 4 + rem4(x + a + 4 - g)

    def reader(block):
        g, a = block
        return rem4(y + 1 + g) * 4 + rem4(x + 4 - a + g)

    others = [(g, a) for g in range(4) for a in range(4)][:-1]

    def greet(**device):
        pl.semaphore_signal(
            pltpu.get_barrier_semaphore(), inc=1, device_id=device, device_id_type=MESH
        )

    for block in others:
        greet(req=reader(block))
    for e in range(1, nkv):
        greet(kvh=lax.rem(mj + e, nkv))

    loads = [
        pltpu.make_async_copy(q_hbm, q_all.at[0], ld_sem.at[0]),
        pltpu.make_async_copy(task_hbm, task_ref, ld_sem.at[1]),
        pltpu.make_async_copy(len_hbm, len_ref, ld_sem.at[2]),
        pltpu.make_async_copy(cv_hbm, vbuf.at[pl.ds(0, corpus)], ld_sem.at[3]),
        pltpu.make_async_copy(tv_hbm, vbuf.at[pl.ds(corpus, keys - corpus)], ld_sem.at[4]),
        pltpu.make_async_copy(ck_hbm, kbuf.at[pl.ds(0, corpus)], ld_sem.at[5]),
        pltpu.make_async_copy(tk_hbm, kbuf.at[pl.ds(corpus, keys - corpus)], ld_sem.at[6]),
        pltpu.make_async_copy(hk_hbm, hkb, ld_sem.at[7]),
        pltpu.make_async_copy(hv_hbm, hvb, ld_sem.at[8]),
        pltpu.make_async_copy(w_hbm, wbuf, ld_sem.at[9]),
    ]
    for c in loads:
        c.start()

    loads[0].wait()
    pl.semaphore_wait(pltpu.get_barrier_semaphore(), nreq + nkv - 2)

    def q_copy(block):
        return pltpu.make_async_remote_copy(
            src_ref=q_all.at[0],
            dst_ref=q_all.at[slot(block)],
            send_sem=q_send,
            recv_sem=q_recv.at[number(block)],
            device_id={"req": reader(block)},
            device_id_type=MESH,
        )

    for block in others:
        q_copy(block).start()

    def head_major(k):
        block = q_all[k]
        return [block[:, h * HD : (h + 1) * HD] for h in range(heads)]

    loads[1].wait()
    lane = lax.broadcasted_iota(jnp.int32, (nreq, nreq * rows), 1)
    row = lax.broadcasted_iota(jnp.int32, (nreq, nreq * rows), 0)
    mine = jnp.broadcast_to(task_ref[...], lane.shape) == me // HOLDERS
    mine = jnp.where(mine & (lane // rows == row), 1.0, 0.0).astype(BF16)
    er = lax.broadcasted_iota(jnp.int32, (nreq * rows, cols), 0)
    ec = lax.broadcasted_iota(jnp.int32, (nreq * rows, cols), 1)
    spread = jnp.where(er % rows == ec % rows, 1.0, 0.0).astype(BF16)
    valid[...] = jnp.dot(mine, spread, preferred_element_type=F32)

    loads[3].wait()
    for c in range(nch):
        if c == ncorp:
            loads[4].wait()
        at = slice(c * chunk, (c + 1) * chunk)
        vt[:HD, at] = vbuf[at, :].T
    vt[HD:, :] = jnp.ones((vt.shape[0] - HD, keys), BF16)
    loads[5].wait()
    loads[6].wait()

    early = nreq - 4

    def arrive(blocks):
        for block in blocks:
            q_copy(block).wait_recv()

    def q_of(blocks):
        return jnp.concatenate([tile for b in blocks for tile in head_major(slot(b))], 0)

    def score(c, q, sref, peaks):
        at = slice(c * chunk, (c + 1) * chunk)
        s = lax.dot_general(kbuf[at, :], q, NT, preferred_element_type=F32)
        sref[at, : s.shape[1]] = s
        part = jnp.max(s.reshape(chunk // 8, 8, s.shape[1]), axis=0)
        g = 0 if c < ncorp else 1
        peaks[g] = part if peaks[g] is None else jnp.maximum(peaks[g], part)

    def weigh(c, sref, pref, shifts):
        at = slice(c * chunk, (c + 1) * chunk)
        n = shifts[0].shape[1]
        p = jnp.exp2(sref[at, :n] * CS - shifts[0 if c < ncorp else 1])
        pref[at, :n] = p.astype(BF16)

    def add_up(g, pref, n, acc):
        at = slice(g * deep, (g + 1) * deep)
        part = jnp.dot(vt[:, at], pref[at, :n], preferred_element_type=F32)
        return part if acc is None else acc + part

    def o_copy(block):
        t = number(block)
        return pltpu.make_async_remote_copy(
            src_ref=osend.at[t],
            dst_ref=orecv.at[t],
            send_sem=o_send,
            recv_sem=o_recv.at[1 if isinstance(t, int) and t >= early else 0],
            device_id={"req": source(block)},
            device_id_type=MESH,
        )

    def pack(lse):
        hi = lse.astype(BF16).astype(F32)
        mid = (lse - hi).astype(BF16).astype(F32)
        lo = lse - hi - mid
        sub = lax.broadcasted_iota(jnp.int32, (16, lse.shape[1]), 0)
        info = jnp.where(sub == 0, hi, jnp.where(sub == 1, mid, jnp.where(sub == 2, lo, 0.0)))
        return info.astype(BF16)

    def unpack(ref, k):
        lse = jnp.sum(ref[k, HD:, :].astype(F32), axis=0, keepdims=True)
        return ref[k, :HD, :].astype(F32), lse

    def merge(parts):
        top = functools.reduce(jnp.maximum, [v for _, v in parts])
        ws = [jnp.exp2(v - top) for _, v in parts]
        den = functools.reduce(jnp.add, ws)
        inv = 1.0 / den
        o = functools.reduce(jnp.add, [o * (w * inv) for (o, _), w in zip(parts, ws)])
        return o, top + jnp.log2(den)

    def go_home(blocks):
        for block in blocks:
            t = number(block)
            if not isinstance(t, int) or t < nreq - 1:
                o_copy(block).start()

    def stage(now, then, s_now, s_then, pref, peaks, alone=True):
        n = len(now) * cols
        mask = jnp.concatenate([valid[pl.ds(source(b), 1), :] for b in now], 1) > 0
        pk = [jnp.max(m, axis=0, keepdims=True) for m in peaks]
        top = jnp.maximum(pk[0], jnp.where(mask, pk[1], -FAR)) * CS
        shifts = [top, jnp.where(mask, top, FAR)]
        later = [None, None]
        if then:
            if alone:
                arrive(then)
            q = q_of(then)
        acc, done = None, 0
        for c in range(nch):
            if then:
                score(c, q, s_then, later)
            weigh(c, s_now, pref, shifts)
            if (done + 1) * per <= c:
                acc = add_up(done, pref, n, acc)
                done += 1
        while done * deep < keys:
            acc = add_up(done, pref, n, acc)
            done += 1
        total = acc[HD : HD + 1, :]
        o = (acc[:HD, :] * (1.0 / total)).astype(BF16)
        info = pack(top + jnp.log2(total))
        for i, block in enumerate(now):
            at = slice(i * cols, (i + 1) * cols)
            t = number(block)
            osend[t, :HD, :] = o[:, at]
            osend[t, HD:, :] = info[:, at]
        if alone:
            go_home(now)
        return later

    def first_scores(blocks, sref):
        peaks = [None, None]
        q = q_of(blocks)
        for c in range(nch):
            score(c, q, sref, peaks)
        return peaks

    stage([(3, 3)], None, sb, None, pb, first_scores([(3, 3)], sb))

    pr = lax.broadcasted_iota(jnp.int32, (cols, cols), 0)
    pc = lax.broadcasted_iota(jnp.int32, (cols, cols), 1)
    perm = jnp.where((pr % heads == pc // rows) & (pr // heads == pc % rows), 1.0, 0.0)
    perm16 = perm.astype(BF16)
    hq[...] = jnp.dot(perm16, jnp.concatenate(head_major(0), 0), preferred_element_type=F32)
    loads[2].wait()
    loads[7].wait()
    hcol = lax.broadcasted_iota(jnp.int32, (heads, hist), 1)
    for r in range(rows):
        at = slice(r * heads, (r + 1) * heads)
        s = lax.dot_general(
            hq[at, :].astype(BF16),
            hkb[r * hist : (r + 1) * hist, :],
            NT,
            preferred_element_type=F32,
        )
        hs[at, :] = jnp.where(hcol < len_ref[r], s, -FAR)
    s = hs[...]
    hm = jnp.max(s, axis=1, keepdims=True)
    p = jnp.exp2((s - hm) * CS)
    htot = jnp.sum(p, axis=1, keepdims=True)
    hs[...] = p
    loads[8].wait()
    for r in range(rows):
        at = slice(r * heads, (r + 1) * heads)
        hq[at, :] = jnp.dot(
            hs[at, :].astype(BF16), hvb[r * hist : (r + 1) * hist, :], preferred_element_type=F32
        )
    ho = (hq[...] * (1.0 / htot)).astype(BF16)
    hot = lax.dot_general(ho, perm16, TN, preferred_element_type=F32)
    hl = jnp.sum(perm * (hm * CS + jnp.log2(htot)), axis=0, keepdims=True)

    arrive([(0, 0), (0, 1)])
    peaks = first_scores([(0, 0), (0, 1)], sa)

    def twice(g, peaks):
        one, two = [(g, 0), (g, 1)], [(g, 2), (g, 3)]
        three = [(g + 1, 0), (g + 1, 1)]
        arrive(two)
        peaks = stage(one, two, sa, sb, pa, list(peaks), alone=False)
        arrive(three)
        peaks = stage(two, three, sb, sa, pb, peaks, alone=False)
        go_home(one + two)
        return tuple(peaks)

    peaks = list(lax.fori_loop(0, 3, twice, tuple(peaks)))
    peaks = stage([(3, 0), (3, 1)], [(3, 2)], sa, sb, pa, peaks)
    stage([(3, 2)], None, sb, None, pb, peaks)

    def arrived(t, n):
        pltpu.make_async_remote_copy(
            src_ref=osend.at[pl.ds(t, n)],
            dst_ref=orecv.at[pl.ds(t, n)],
            send_sem=o_send,
            recv_sem=o_recv.at[t // early],
            device_id={"req": source((0, 0))},
            device_id_type=MESH,
        ).wait_recv()

    arrived(0, early)
    home = merge(
        [unpack(osend, nreq - 1), (hot, hl)] + [unpack(orecv, t) for t in range(early)]
    )
    arrived(early, 3)
    att, _ = merge([home] + [unpack(orecv, t) for t in range(early, nreq - 1)])
    att = att.T.astype(BF16)
    att = jnp.concatenate([att[h * rows : (h + 1) * rows, :] for h in range(heads)], 1)

    loads[9].wait()

    def kv_peer(e):
        if isinstance(e, int):
            dz, dc = (0, 1, 3, 2)[e // 2], e % 2
        else:
            half, dc = lax.div(e, 2), lax.rem(e, 2)
            dz = half + lax.div(half, 2) - 2 * lax.div(half, 3)
        return lax.rem(mz + dz, 4) * 2 + lax.rem(mc + dc, 2)

    def p_copy(e):
        return pltpu.make_async_remote_copy(
            src_ref=psend.at[e],
            dst_ref=out_ref.at[e],
            send_sem=p_send,
            recv_sem=p_recv,
            device_id={"kvh": kv_peer(e)},
            device_id_type=MESH,
        )

    def project(e):
        at = pl.ds(pl.multiple_of(kv_peer(e) * out_w, out_w), out_w)
        return jnp.dot(att, wbuf[:, at], preferred_element_type=F32)

    def send_p(i, carry):
        e = nkv - 1 - i
        psend[e] = project(e).astype(BF16)
        p_copy(e).start()
        return carry

    lax.fori_loop(0, nkv - 1, send_p, 0)
    psend[0] = project(0).astype(BF16)
    keep = pltpu.make_async_copy(psend.at[0], out_ref.at[0], ld_sem.at[1])
    keep.start()

    def whole(src, dst, send_sem, recv_sem):
        return pltpu.make_async_remote_copy(
            src_ref=src,
            dst_ref=dst,
            send_sem=send_sem,
            recv_sem=recv_sem,
            device_id={"kvh": kv_peer(1)},
            device_id_type=MESH,
        )

    most = pl.ds(0, nreq - 1)
    whole(q_all.at[most], q_all.at[most], q_send, q_recv.at[0]).wait_send()
    whole(osend.at[most], orecv.at[most], o_send, o_recv.at[0]).wait_send()
    parts = whole(psend.at[pl.ds(1, nkv - 1)], out_ref.at[pl.ds(1, nkv - 1)], p_send, p_recv)
    parts.wait_send()
    parts.wait_recv()
    keep.wait()


def solution(mesh):
    nreq, nkv = mesh.shape["req"], mesh.shape["kvh"]

    def shards(q, ck, cv, tk, tv, hk, hv, lengths, task_of, w):
        rows, width = q.shape
        cols = rows * (width // HD)
        keys = ck.shape[0] + tk.shape[0]
        hist = hk.shape[0] // rows
        out_w = w.shape[1] // nkv
        hbm = pl.BlockSpec(memory_space=pl.ANY)
        dma = pltpu.SemaphoreType.DMA
        parts = pl.pallas_call(
            kernel,
            out_shape=jax.ShapeDtypeStruct((nkv, rows, out_w), BF16),
            in_specs=[hbm] * 10,
            out_specs=hbm,
            scratch_shapes=[
                pltpu.VMEM((nreq, rows, width), BF16),
                pltpu.VMEM((keys, HD), BF16),
                pltpu.VMEM((keys, HD), BF16),
                pltpu.VMEM((HD + 16, keys), BF16),
                pltpu.VMEM(hk.shape, BF16),
                pltpu.VMEM(hv.shape, BF16),
                pltpu.SMEM(lengths.shape, jnp.int32),
                pltpu.VMEM((1, nreq * rows), jnp.int32),
                pltpu.VMEM(w.shape, BF16),
                pltpu.VMEM((keys, 2 * cols), F32),
                pltpu.VMEM((keys, 2 * cols), F32),
                pltpu.VMEM((keys, 2 * cols), BF16),
                pltpu.VMEM((keys, 2 * cols), BF16),
                pltpu.VMEM((nreq, HD + 16, cols), BF16),
                pltpu.VMEM((nreq, HD + 16, cols), BF16),
                pltpu.VMEM((cols, hist), F32),
                pltpu.VMEM((cols, HD), F32),
                pltpu.VMEM((nreq, cols), F32),
                pltpu.VMEM((nkv, rows, out_w), BF16),
                dma((10,)),
                dma,
                dma((nreq - 1,)),
                dma,
                dma((2,)),
                dma,
                dma,
            ],
            compiler_params=pltpu.CompilerParams(
                collective_id=0, has_side_effects=True, vmem_limit_bytes=60 * 2**20
            ),
        )(q, ck, cv, tk, tv, hk, hv, lengths, task_of.reshape(1, -1), w)
        return jnp.sum(parts.astype(F32), axis=0).astype(BF16)

    return jax.shard_map(
        shards,
        mesh=mesh,
        in_specs=(P("req", "kvh"),) * 7 + (P("req"), P(), P("kvh", None)),
        out_specs=P("req", "kvh"),
        check_vma=False,
    )
```
